256 devices in a mesh: fsdp: 32 (over x, y, core), tp: 8 (over z).
Axes of the slice: x: 4, y: 4, z: 8, core: 2. Of those that a mesh axis runs over, the one named last changes fastest.
Arguments:
- tokens: bfloat16 [8192, 4096], P('fsdp'), may hold values from -6 to 6
- cotangent: bfloat16 [8192, 7168], P('fsdp', 'tp'), may hold values from -6 to 6
- gate_weight: bfloat16 [4096, 7168], P('fsdp', 'tp'), may hold values from -4 to 4
- up_weight: bfloat16 [4096, 7168], P('fsdp', 'tp'), may hold values from -4 to 4
Outputs:
- input_grad: bfloat16 [8192, 4096], P('fsdp', 'tp')
- gate_grad: bfloat16 [4096, 7168], P('fsdp', 'tp')
- up_grad: bfloat16 [4096, 7168], P('fsdp', 'tp')
- weight_amax: float32 [2], replicated
The draws below stay inside these ranges and needn't reach their ends.
All inputs are finite; a program needn't handle non-finite values. Where the reference program divides by a largest or mean magnitude, that divisor is 1e-20 or more.
Results may differ from the reference program's by a relative error of at most 0.019.
Values may be sent and summed in bfloat16 or wider, within the bound.
A program may use at most 128 MiB of HBM per device.

```python
import jax
import jax.numpy as jnp
from jax import lax

D = 4096
TOK_DEV = 256
FF = 7168
TOKENS = 8192
N_FSDP = 32


def scaled_matrix(key):
    first, second, third = jax.random.split(key, 3)
    overall = jnp.exp(jax.random.uniform(first, (), jnp.float32, -0.7, 0.7))
    row_scale = jnp.exp(jax.random.uniform(third, (D, 1), jnp.float32, -0.5, 0.5))
    base = jnp.clip(jax.random.normal(second, (D, FF), jnp.float32), -6.0, 6.0)
    return base * row_scale * overall * D ** (-0.5)


def draw_gate_weight(key, part):
    key = jax.random.fold_in(key, 11)
    return scaled_matrix(key).astype(jnp.bfloat16)


def draw_up_weight(key, part):
    key = jax.random.fold_in(key, 23)
    return scaled_matrix(key).astype(jnp.bfloat16)


def raised(result, key, source, target, parts, factor):
    owner, partner = [(jnp.arange(result.shape[axis_at]) // (result.shape[axis_at] // parts)).reshape([-1 if axis == axis_at else 1 for axis in range(result.ndim)]) for axis_at in (source, target)]
    chosen = jax.random.permutation(key, parts)[partner]
    strong = (owner == chosen) | (owner == (partner + parts // 2) % parts)
    return jnp.where(strong, factor * result, result)


def shard_levels(rng, dims, pieces, least, high):
    def one(axis_at, parts):
        draws = jax.random.uniform(jax.random.fold_in(jax.random.fold_in(rng, 6), axis_at), (parts,), jnp.float32, least / len(pieces), high / len(pieces))
        return jnp.repeat(jnp.exp(draws), dims[axis_at] // parts).reshape((-1,) + (1,) * (len(dims) - axis_at - 1))

    loudness = one(*pieces[0])
    for cut in pieces[1:]:
        loudness = loudness * one(*cut)
    return loudness


def gaussian(key, extent, scale, most, pieces=(), dtype=jnp.bfloat16):
    level = shard_levels(key, extent, pieces, -0.22, 0.18) if pieces else 1.0
    entries = jax.random.normal(key, extent, jnp.float32) * scale * level
    return jnp.minimum(jnp.maximum(entries, -most), most).astype(dtype)


def gaussian_with(own_key, dims, deviation, most, shards, heavy, kind=jnp.bfloat16):
    array = deviation * jax.random.normal(own_key, dims, jnp.float32)
    if shards:
        array = array * shard_levels(own_key, dims, shards, -0.22, 0.18)
    return jnp.clip(raised(array, jax.random.fold_in(own_key, 3), *heavy), -most, most).astype(kind)


def setup_inputs(seed: int = 0) -> dict:
    streams_of = jax.random.split(jax.random.key(seed), 5)
    return {
        "tokens": gaussian_with(streams_of[0], (TOKENS, D), 1.0, 6.0, ((0, 32),), (0, 1, 32, 2.75)),
        "cotangent": gaussian(streams_of[1], (TOKENS, FF), 1.0, 6.0, ((0, 32), (1, 8))),
        "gate_weight": draw_gate_weight(jax.random.fold_in(streams_of[4], 71), 0),
        "up_weight": draw_up_weight(jax.random.fold_in(streams_of[4], 71), 0),
    }


def quantize(weight):
    amax = jnp.max(jnp.abs(weight.astype(jnp.float32)))
    scale = 448.0 / (amax + 1e-6)
    scaled = (weight.astype(jnp.float32) * scale).astype(jnp.bfloat16)
    return amax, scale, scaled


def reference(tokens, cotangent, gate_weight, up_weight):
    amax_gate, scale_gate, q_gate = quantize(gate_weight)
    amax_up, scale_up, q_up = quantize(up_weight)
    gate = jnp.dot(tokens, q_gate, preferred_element_type=jnp.float32) / scale_gate
    up = jnp.dot(tokens, q_up, preferred_element_type=jnp.float32) / scale_up
    sig = jax.nn.sigmoid(gate)
    cot = cotangent.astype(jnp.float32)
    grad_gate = (cot * up * sig * (1.0 + gate * (1.0 - sig))).astype(jnp.bfloat16)
    grad_up = (cot * gate * sig).astype(jnp.bfloat16)
    input_grad = (jnp.dot(grad_gate, q_gate.T, preferred_element_type=jnp.float32) / scale_gate
                  + jnp.dot(grad_up, q_up.T, preferred_element_type=jnp.float32) / scale_up).astype(jnp.bfloat16)
    token_blocks = tokens.reshape(N_FSDP, TOK_DEV, D)
    gate_blocks = grad_gate.reshape(N_FSDP, TOK_DEV, FF)
    up_blocks = grad_up.reshape(N_FSDP, TOK_DEV, FF)

    def add_block(carry, block):
        xpart, gpart, upart = block
        gsum = jnp.dot(xpart.T, gpart, preferred_element_type=jnp.float32).astype(jnp.bfloat16)
        usum = jnp.dot(xpart.T, upart, preferred_element_type=jnp.float32).astype(jnp.bfloat16)
        gsum, usum = lax.optimization_barrier((gsum, usum))
        return (carry[0] + gsum.astype(jnp.float32), carry[1] + usum.astype(jnp.float32)), None

    zeros = jnp.zeros((D, FF), jnp.float32)
    totals, unused = lax.scan(add_block, (zeros, zeros), (token_blocks, gate_blocks, up_blocks))
    gate_grad = totals[0].astype(jnp.bfloat16)
    up_grad = totals[1].astype(jnp.bfloat16)
    weight_amax = jnp.stack([amax_gate, amax_up]).astype(jnp.float32)
    return input_grad, gate_grad, up_grad, weight_amax
```

```python
import jax
import jax.numpy as jnp
from jax import lax
from jax.experimental import pallas as pl
from jax.experimental.pallas import tpu as pltpu
from jax.sharding import PartitionSpec as P

MESH = pl.DeviceIdType.MESH
F32 = jnp.float32
BF16 = jnp.bfloat16
SIDE = 4
DEPTH = 8
ROWS = 128
HALF = ROWS // 2
CHIP_ROWS = 2 * ROWS
TOK = 256
D = 4096
WIDTH = 896
MAIN = 384
ZCOL = D // DEPTH
NT = (((1,), (1,)), ((), ()))


def kernel(
    tok_ref, cot_ref, wg_ref, wu_ref,
    ig_ref, gg_ref, ug_ref, amax_ref,
    xs, xt, cots, wraw, wq, h, g, gs, psib, scales, am_mine, am_in,
    s1buf, s1in, s2buf, s2in, rbuf, t1in, t2in, final, final_in,
    p_own, p_send, p_in, z1in, zin,
    loc_sem, pair_send, pair_recv, ag_send, ag_recv, am_send, am_recv,
    s1_send, s1_recv, s2_send, s2_recv, t1_send, t1_recv, t2_send, t2_recv,
    p_ssem, p_rsem, z1_send, z1_recv, z_send, z_recv,
):
    f = lax.axis_index("fsdp")
    z = lax.axis_index("tp")
    c = lax.rem(f, 2)
    chip = lax.div(f, 2)
    x = lax.div(chip, SIDE)
    y = lax.rem(chip, SIDE)

    def chip_at(dx, dy):
        return lax.rem(x + dx, SIDE) * SIDE + lax.rem(y + dy, SIDE)

    def at(dx, dy):
        return (chip_at(dx, dy) * 2 + c, z)

    def at_z(dz):
        return (f, lax.rem(z + dz, DEPTH))

    sibling = (chip * 2 + 1 - c, z)

    def place(r, a, b):
        return (a, b) if r == 0 else (b, a)

    def row_of(r, a, b):
        return pl.multiple_of(chip_at(*place(r, a, b)) * CHIP_ROWS + (c if r == 0 else 1 - c) * ROWS, ROWS)

    def remote(src, dst, ssem, rsem, device):
        return pltpu.make_async_remote_copy(
            src_ref=src, dst_ref=dst, send_sem=ssem, recv_sem=rsem, device_id=device, device_id_type=MESH
        )

    barrier = pltpu.get_barrier_semaphore()
    peers = [at(k, 0) for k in (1, 2, 3)] + [at(0, k) for k in (1, 2, 3)]
    peers += [at_z(k) for k in range(1, DEPTH)] + [sibling]
    for peer in peers:
        pl.semaphore_signal(barrier, inc=1, device_id=peer, device_id_type=MESH)

    tok_local = pltpu.make_async_copy(tok_ref, xs.at[pl.ds(0, TOK)], loc_sem.at[0])
    tok_local.start()
    cot_local = pltpu.make_async_copy(cot_ref, cots.at[pl.ds(0, TOK)], loc_sem.at[1])
    cot_local.start()

    lane = lax.broadcasted_iota(jnp.int32, (ROWS, 128), 1)
    low = lane < 64

    def packed_mixed(core):
        g3 = wg_ref[:, MAIN : MAIN + 128].astype(F32)
        u3 = wu_ref[:, MAIN : MAIN + 128].astype(F32)
        first = jnp.where(low, g3, pltpu.roll(u3, 64, 1))
        second = jnp.where(low, pltpu.roll(g3, 64, 1), u3)
        return jnp.where(core == 0, first, second).astype(BF16)

    own_rows = pl.ds(row_of(0, 0, 0), ROWS)
    sib_rows = pl.ds(row_of(1, 0, 0), ROWS)
    own_cols = pl.ds(pl.multiple_of(c * 512, 128), MAIN)
    sib_cols = pl.ds(pl.multiple_of((1 - c) * 512, 128), MAIN)
    psib[:, 0:MAIN] = wg_ref[:, sib_cols]
    psib[:, MAIN : 2 * MAIN] = wu_ref[:, sib_cols]
    psib[:, 2 * MAIN : WIDTH] = packed_mixed(1 - c)
    wraw[own_rows, 0:MAIN] = wg_ref[:, own_cols]
    wraw[own_rows, MAIN : 2 * MAIN] = wu_ref[:, own_cols]
    wraw[own_rows, 2 * MAIN : WIDTH] = packed_mixed(c)

    pl.semaphore_wait(barrier, len(peers))

    swap = remote(psib, wraw.at[own_rows], pair_send.at[0], pair_recv.at[0], sibling)
    swap.start()

    def ag_copy(r, slot, a, b, part, axis, sign):
        rows = row_of(r, a, b)
        if part is None:
            rows, count = rows, ROWS
        else:
            rows, count = rows + part * HALF, HALF
        ref = wraw.at[pl.ds(pl.multiple_of(rows, HALF), count)]
        step = (sign % SIDE, 0) if axis == 0 else (0, sign % SIDE)
        return remote(ref, ref, ag_send.at[r, slot], ag_recv.at[r, slot], at(*place(r, *step)))

    started = []

    def ag_start(*args):
        copy = ag_copy(*args)
        copy.start()
        started.append(copy)

    def ag_wait(r, slot, a, b, part):
        ag_copy(r, slot, a, b, part, 0, 1).wait_recv()

    def first_start(r):
        ag_start(r, 1, 0, 0, None, 0, 1)
        ag_start(r, 0, 0, 0, None, 0, -1)

    def second_start(r, a):
        ag_start(r, 4 + 4 * a + 1, a, 0, None, 1, 1)
        ag_start(r, 4 + 4 * a, a, 0, None, 1, -1)

    def second_forward(r, a):
        ag_wait(r, 4 + 4 * a + 1, a, 3, None)
        ag_start(r, 4 + 4 * a + 2, a, 3, 0, 1, 1)
        ag_wait(r, 4 + 4 * a, a, 1, None)
        ag_start(r, 4 + 4 * a + 3, a, 1, 1, 1, -1)

    def second_end(r, a):
        ag_wait(r, 4 + 4 * a + 2, a, 2, 0)
        ag_wait(r, 4 + 4 * a + 3, a, 2, 1)

    first_start(0)
    second_start(0, 0)
    tok_pair = remote(tok_ref, xs.at[pl.ds(TOK, TOK)], pair_send.at[1], pair_recv.at[1], sibling)
    cot_pair = remote(cot_ref, cots.at[pl.ds(TOK, TOK)], pair_send.at[2], pair_recv.at[2], sibling)
    remote(psib, wraw.at[sib_rows], pair_send.at[0], pair_recv.at[0], sibling).wait_recv()
    first_start(1)
    second_start(1, 0)
    tok_pair.start()
    cot_pair.start()

    am_rows = lax.broadcasted_iota(jnp.int32, (8, 128), 0)

    def largest(ref):
        return jnp.max(jnp.abs(ref[...].astype(F32)), keepdims=True)

    am_mine[0] = jnp.where(am_rows < 4, largest(wg_ref), largest(wu_ref))
    stages = [
        [(at(k, 0), k - 1) for k in (1, 2, 3)],
        [(at(0, k), k + 2) for k in (1, 2, 3)],
        [(at_z(k), k + 5) for k in range(1, DEPTH)],
        [(sibling, 13)],
    ]

    def am_copies(stage):
        return [
            remote(am_mine.at[stage], am_in.at[slot], am_send.at[slot], am_recv.at[slot], device)
            for device, slot in stages[stage]
        ]

    def am_start(stage):
        for copy in am_copies(stage):
            copy.start()

    def am_finish(stage):
        best = am_mine[stage]
        for copy in am_copies(stage):
            copy.wait_recv()
        for _, slot in stages[stage]:
            best = jnp.maximum(best, am_in[slot])
        am_mine[stage + 1] = best

    am_start(0)

    for r in (0, 1):
        ag_wait(r, 1, 3, 0, None)
        ag_start(r, 2, 3, 0, 0, 0, 1)
        ag_wait(r, 0, 1, 0, None)
        ag_start(r, 3, 1, 0, 1, 0, -1)
    for r in (0, 1):
        second_start(r, 1)
        second_start(r, 3)
    am_finish(0)
    am_start(1)
    for r in (0, 1):
        second_forward(r, 0)
    am_finish(1)
    am_start(2)
    for r in (0, 1):
        ag_wait(r, 2, 2, 0, 0)
        ag_wait(r, 3, 2, 0, 1)
        second_start(r, 2)
    am_finish(2)
    am_start(3)
    am_finish(3)

    gate_max = jnp.max(am_mine[4, 0:4, :])
    up_max = jnp.max(am_mine[4, 4:8, :])
    amax_ref[0] = gate_max
    amax_ref[1] = up_max
    col = lax.broadcasted_iota(jnp.int32, (8, WIDTH), 1)
    is_gate = (col < MAIN) | ((col >= 2 * MAIN) & (col < 2 * MAIN + 64))
    scale = 448.0 / (jnp.where(is_gate, gate_max, up_max) + 1e-06)
    scales[0] = scale
    scales[1] = 1.0 / scale

    tok_local.wait()
    cot_local.wait()
    tok_pair.wait_recv()
    cot_pair.wait_recv()

    h[...] = jnp.zeros_like(h)

    def chunk(dx, dy):
        start = pl.multiple_of(chip_at(dx, dy) * CHIP_ROWS, CHIP_ROWS)
        rows = pl.ds(start, CHIP_ROWS)
        wq[rows] = (wraw[rows].astype(F32) * scales[0, 0:1, :]).astype(BF16)

        @pl.loop(0, 2)
        def _(m):
            toks = pl.ds(pl.multiple_of(m * TOK, TOK), TOK)
            h[toks] += jnp.dot(xs[toks, rows], wq[rows], preferred_element_type=F32)

    chunk(0, 0)

    @pl.loop(0, 4)
    def _(k):
        along = 1 + 2 * lax.rem(k, 2)
        chunk(along * (1 - lax.div(k, 2)), along * lax.div(k, 2))

    @pl.loop(0, D // 128)
    def _(b):
        cols = pl.ds(pl.multiple_of(b * 128, 128), 128)
        xt[cols, :] = xs[:, cols].T

    for a in (1, 3):
        for r in (0, 1):
            second_forward(r, a)
    for r in (0, 1):
        second_end(r, 0)

    @pl.loop(0, 2)
    def _(k):
        chunk(2 * k, 2 * (1 - k))

    for r in (0, 1):
        second_forward(r, 2)

    @pl.loop(0, 4)
    def _(k):
        chunk(1 + 2 * lax.rem(k, 2), 1 + 2 * lax.div(k, 2))

    for a in (1, 3):
        for r in (0, 1):
            second_end(r, a)

    @pl.loop(0, 4)
    def _(k):
        along = 1 + 2 * lax.rem(k, 2)
        flip = lax.div(k, 2)
        chunk(2 * flip + along * (1 - flip), 2 * (1 - flip) + along * flip)

    for r in (0, 1):
        second_end(r, 2)
    chunk(2, 2)

    low_tok = lax.broadcasted_iota(jnp.int32, (64, 128), 1) < 64

    def activation_grads(gate, up, cot):
        sig = jax.nn.sigmoid(gate)
        return cot * up * sig * (1.0 + gate * (1.0 - sig)), cot * gate * sig

    @pl.loop(0, 2 * TOK // 64)
    def _(m):
        toks = pl.ds(pl.multiple_of(m * 64, 64), 64)
        inv = scales[1, 0:1, :]
        hidden = h[toks] * inv
        cot = cots[toks, pl.ds(pl.multiple_of(c * 512, 128), MAIN)].astype(F32)
        dgate, dup = activation_grads(hidden[:, 0:MAIN], hidden[:, MAIN : 2 * MAIN], cot)
        mixed = hidden[:, 2 * MAIN : WIDTH]
        block = cots[toks, MAIN : MAIN + 128].astype(F32)
        block = jnp.where(c == 0, block, pltpu.roll(block, 64, 1))
        mgate, mup = activation_grads(mixed, pltpu.roll(mixed, 64, 1), block)
        both = jnp.where(low_tok, mgate, pltpu.roll(mup, 64, 1))
        for cols, part in ((slice(0, MAIN), dgate), (slice(MAIN, 2 * MAIN), dup), (slice(2 * MAIN, WIDTH), both)):
            g[toks, cols] = part.astype(BF16)
            gs[toks, cols] = (part * inv[:, cols]).astype(BF16)

    def weight_grad(r, a, b):
        return jnp.dot(xt[pl.ds(row_of(r, a, b), ROWS)], g[...], preferred_element_type=F32)

    def toward(r, axis, sign):
        return at(*place(r, *((sign % SIDE, 0) if axis == 0 else (0, sign % SIDE))))

    def s1_copy(r, a, part):
        return remote(
            s1buf.at[r, a, pl.ds(part * HALF, HALF)], s1in.at[r, a, part],
            s1_send.at[r, a, part], s1_recv.at[r, a, part], toward(r, 1, 1 - 2 * part),
        )

    def s2_copy(r, a, part):
        return remote(
            s2buf.at[r, a, part], s2in.at[r, a, part],
            s2_send.at[r, a, part], s2_recv.at[r, a, part], toward(r, 1, 1 - 2 * part),
        )

    def t1_copy(r, part):
        return remote(
            rbuf.at[r, 2, pl.ds(part * HALF, HALF)], t1in.at[r, part],
            t1_send.at[r, part], t1_recv.at[r, part], toward(r, 0, 1 - 2 * part),
        )

    def t2_copy(r, part):
        return remote(
            rbuf.at[r, 1 + 2 * part], t2in.at[r, part],
            t2_send.at[r, part], t2_recv.at[r, part], toward(r, 0, 1 - 2 * part),
        )

    for a in (2, 1, 3, 0):
        for r in (0, 1):
            s1buf[r, a] = weight_grad(r, a, 2).astype(BF16)
            s1_copy(r, a, 0).start()
            s1_copy(r, a, 1).start()

    def p_copy(dz):
        return remote(p_send.at[dz], p_in.at[dz], p_ssem.at[dz], p_rsem.at[dz], sibling)

    @pl.loop(0, DEPTH)
    def _(k):
        odd = lax.rem(k, 2)
        dz = odd * (4 - lax.div(k + 1, 2)) + (1 - odd) * (4 + lax.div(k, 2))
        cols = pl.ds(pl.multiple_of(lax.rem(z + dz, DEPTH) * ZCOL, ZCOL), ZCOL)
        p_send[dz] = lax.dot_general(gs[TOK:, :], wq[cols], NT, preferred_element_type=F32).astype(BF16)
        p_copy(dz).start()
        p_own[dz] = lax.dot_general(gs[:TOK, :], wq[cols], NT, preferred_element_type=F32).astype(BF16)

    def step2(a):
        for r in (0, 1):
            for part in (0, 1):
                s1_copy(r, a, part).wait_recv()
                lo = slice(part * HALF, part * HALF + HALF)
                hi = slice((1 - part) * HALF, (1 - part) * HALF + HALF)
                grad = weight_grad(r, a, 1 + 2 * part)
                s2buf[r, a, part, lo] = (grad[lo] + s1in[r, a, part].astype(F32)).astype(BF16)
                s2buf[r, a, part, hi] = grad[hi].astype(BF16)
                s2_copy(r, a, part).start()

    def reduced(r, a):
        s2_copy(r, a, 0).wait_recv()
        s2_copy(r, a, 1).wait_recv()
        return weight_grad(r, a, 0) + s2in[r, a, 0].astype(F32) + s2in[r, a, 1].astype(F32)

    def z1_copy(part):
        return remote(
            p_own.at[4, pl.ds(part * (TOK // 2), TOK // 2)], z1in.at[part],
            z1_send.at[part], z1_recv.at[part], at_z(1 if part == 0 else DEPTH - 1),
        )

    def z_copy(step, part):
        dz = (3 - step) if part == 0 else (5 + step)
        return remote(
            p_own.at[dz], zin.at[step, part],
            z_send.at[step, part], z_recv.at[step, part], at_z(1 if part == 0 else DEPTH - 1),
        )

    def pair_sum(dz):
        p_copy(dz).wait_recv()
        return p_own[dz].astype(F32) + p_in[dz].astype(F32)

    def z_first():
        p_own[4] = pair_sum(4).astype(BF16)
        z1_copy(0).start()
        z1_copy(1).start()

    def z_round(step):
        for part in (0, 1):
            dz = (3 - step) if part == 0 else (5 + step)
            total = pair_sum(dz)
            if step == 0:
                z1_copy(part).wait_recv()
                lo = slice(part * (TOK // 2), (part + 1) * (TOK // 2))
                hi = slice((1 - part) * (TOK // 2), (2 - part) * (TOK // 2))
                p_own[dz, lo] = (total[lo] + z1in[part].astype(F32)).astype(BF16)
                p_own[dz, hi] = total[hi].astype(BF16)
            else:
                z_copy(step - 1, part).wait_recv()
                p_own[dz] = (total + zin[step - 1, part].astype(F32)).astype(BF16)
            z_copy(step, part).start()

    step2(2)
    z_first()
    step2(1)
    step2(3)
    z_round(0)
    for r in (0, 1):
        rbuf[r, 2] = reduced(r, 2).astype(BF16)
        t1_copy(r, 0).start()
        t1_copy(r, 1).start()
    step2(0)
    z_round(1)
    for part in (0, 1):
        for r in (0, 1):
            total = reduced(r, 1 + 2 * part)
            t1_copy(r, part).wait_recv()
            lo = slice(part * HALF, part * HALF + HALF)
            hi = slice((1 - part) * HALF, (1 - part) * HALF + HALF)
            rbuf[r, 1 + 2 * part, lo] = (total[lo] + t1in[r, part].astype(F32)).astype(BF16)
            rbuf[r, 1 + 2 * part, hi] = total[hi].astype(BF16)
            t2_copy(r, part).start()
    z_round(2)
    total = pair_sum(0)
    z_copy(2, 0).wait_recv()
    z_copy(2, 1).wait_recv()
    ig_ref[...] = (total + zin[2, 0].astype(F32) + zin[2, 1].astype(F32)).astype(BF16)

    def finished(r):
        total = reduced(r, 0)
        t2_copy(r, 0).wait_recv()
        t2_copy(r, 1).wait_recv()
        return (total + t2in[r, 0].astype(F32) + t2in[r, 1].astype(F32)).astype(BF16)

    final[1] = finished(1)
    last = remote(final.at[1], final_in, pair_send.at[3], pair_recv.at[3], sibling)
    last.start()
    final[0] = finished(0)
    gg_ref[:, own_cols] = final[0, :, 0:MAIN]
    ug_ref[:, own_cols] = final[0, :, MAIN : 2 * MAIN]
    last.wait_recv()
    gg_ref[:, sib_cols] = final_in[:, 0:MAIN]
    ug_ref[:, sib_cols] = final_in[:, MAIN : 2 * MAIN]
    mine = final[0, :, 2 * MAIN : WIDTH].astype(F32)
    theirs = final_in[:, 2 * MAIN : WIDTH].astype(F32)
    first = jnp.where(c == 0, mine, theirs)
    second = jnp.where(c == 0, theirs, mine)
    gg_ref[:, MAIN : MAIN + 128] = jnp.where(low, first, pltpu.roll(second, 64, 1)).astype(BF16)
    ug_ref[:, MAIN : MAIN + 128] = jnp.where(low, pltpu.roll(first, 64, 1), second).astype(BF16)

    swap.wait_send()
    tok_pair.wait_send()
    cot_pair.wait_send()
    for copy in started:
        copy.wait_send()
    for stage in range(4):
        for copy in am_copies(stage):
            copy.wait_send()
    for r in (0, 1):
        for part in (0, 1):
            for a in range(SIDE):
                s1_copy(r, a, part).wait_send()
                s2_copy(r, a, part).wait_send()
            t1_copy(r, part).wait_send()
            t2_copy(r, part).wait_send()
    for dz in range(DEPTH):
        p_copy(dz).wait_send()
    for part in (0, 1):
        z1_copy(part).wait_send()
        for step in range(3):
            z_copy(step, part).wait_send()
    last.wait_send()


def on_device(tokens, cotangent, gate_weight, up_weight):
    vmem = pltpu.VMEM
    dma = pltpu.SemaphoreType.DMA
    piece = (ROWS, WIDTH)
    scratch = [
        vmem((2 * TOK, D), BF16),
        vmem((D, 2 * TOK), BF16),
        vmem((2 * TOK, WIDTH), BF16),
        vmem((D, WIDTH), BF16),
        vmem((D, WIDTH), BF16),
        vmem((2 * TOK, WIDTH), F32),
        vmem((2 * TOK, WIDTH), BF16),
        vmem((2 * TOK, WIDTH), BF16),
        vmem(piece, BF16),
        vmem((2, 8, WIDTH), F32),
        vmem((5, 8, 128), F32),
        vmem((14, 8, 128), F32),
        vmem((2, SIDE) + piece, BF16),
        vmem((2, SIDE, 2, HALF, WIDTH), BF16),
        vmem((2, SIDE, 2) + piece, BF16),
        vmem((2, SIDE, 2) + piece, BF16),
        vmem((2, SIDE) + piece, BF16),
        vmem((2, 2, HALF, WIDTH), BF16),
        vmem((2, 2) + piece, BF16),
        vmem((2,) + piece, BF16),
        vmem(piece, BF16),
        vmem((DEPTH, TOK, ZCOL), BF16),
        vmem((DEPTH, TOK, ZCOL), BF16),
        vmem((DEPTH, TOK, ZCOL), BF16),
        vmem((2, TOK // 2, ZCOL), BF16),
        vmem((3, 2, TOK, ZCOL), BF16),
        dma((2,)), dma((4,)), dma((4,)), dma((2, 20)), dma((2, 20)), dma((14,)), dma((14,)),
        dma((2, SIDE, 2)), dma((2, SIDE, 2)), dma((2, SIDE, 2)), dma((2, SIDE, 2)),
        dma((2, 2)), dma((2, 2)), dma((2, 2)), dma((2, 2)),
        dma((DEPTH,)), dma((DEPTH,)), dma((2,)), dma((2,)), dma((3, 2)), dma((3, 2)),
    ]
    whole = pl.BlockSpec(memory_space=pltpu.VMEM)
    outs = pl.pallas_call(
        kernel,
        out_shape=(
            jax.ShapeDtypeStruct((TOK, ZCOL), BF16),
            jax.ShapeDtypeStruct((ROWS, WIDTH), BF16),
            jax.ShapeDtypeStruct((ROWS, WIDTH), BF16),
            jax.ShapeDtypeStruct((2,), F32),
        ),
        in_specs=[pl.BlockSpec(memory_space=pl.ANY)] * 2 + [whole] * 2,
        out_specs=(whole, whole, whole, pl.BlockSpec(memory_space=pltpu.SMEM)),
        scratch_shapes=scratch,
        compiler_params=pltpu.CompilerParams(
            collective_id=0, has_side_effects=True, vmem_limit_bytes=62 * 1024 * 1024
        ),
        cost_estimate=pl.CostEstimate(flops=3 * 2 * 512 * 4096 * 896, bytes_accessed=4 << 20, transcendentals=512 * 448),
        name="swiglu_backward",
    )(tokens, cotangent, gate_weight, up_weight)
    return outs


def solution(mesh):
    in_specs = (P("fsdp", None), P("fsdp", "tp"), P("fsdp", "tp"), P("fsdp", "tp"))
    out_specs = (P("fsdp", "tp"), P("fsdp", "tp"), P("fsdp", "tp"), P())
    return jax.shard_map(
        on_device, mesh=mesh, in_specs=in_specs, out_specs=out_specs, check_vma=False
    )
```

```python
import jax
import jax.numpy as jnp
from jax import lax
from jax.experimental import pallas as pl
from jax.experimental.pallas import tpu as pltpu
from jax.sharding import PartitionSpec as P

MESH = pl.DeviceIdType.MESH
F32 = jnp.float32
BF16 = jnp.bfloat16
SIDE = 4
DEPTH = 8
ROWS = 128
HALF = ROWS // 2
CHIP_ROWS = 2 * ROWS
TOK = 256
D = 4096
WIDTH = 896
MAIN = 384
ZCOL = D // DEPTH
NT = (((1,), (1,)), ((), ()))


def kernel(
    tok_ref, cot_ref, wg_ref, wu_ref,
    ig_ref, gg_ref, ug_ref, amax_ref,
    xs, xt, cots, wraw, wq, h, g, gs, psib, scales, am_mine, am_in,
    s1buf, s1in, s2buf, s2in, rbuf, t1in, t2in, final, final_in,
    p_own, p_send, p_in, z1in, zin,
    loc_sem, pair_send, pair_recv, ag_send, ag_recv, am_send, am_recv,
    s1_send, s1_recv, s2_send, s2_recv, t1_send, t1_recv, t2_send, t2_recv,
    p_ssem, p_rsem, z1_send, z1_recv, z_send, z_recv,
):
    f = lax.axis_index("fsdp")
    z = lax.axis_index("tp")
    c = lax.rem(f, 2)
    chip = lax.div(f, 2)
    x = lax.div(chip, SIDE)
    y = lax.rem(chip, SIDE)

    def chip_at(dx, dy):
        return lax.rem(x + dx, SIDE) * SIDE + lax.rem(y + dy, SIDE)

    def at(dx, dy):
        return (chip_at(dx, dy) * 2 + c, z)

    def at_z(dz):
        return (f, lax.rem(z + dz, DEPTH))

    sibling = (chip * 2 + 1 - c, z)

    def place(r, a, b):
        return (a, b) if r == 0 else (b, a)

    def row_of(r, a, b):
        return pl.multiple_of(chip_at(*place(r, a, b)) * CHIP_ROWS + (c if r == 0 else 1 - c) * ROWS, ROWS)

    def remote(src, dst, ssem, rsem, device):
        return pltpu.make_async_remote_copy(
            src_ref=src, dst_ref=dst, send_sem=ssem, recv_sem=rsem, device_id=device, device_id_type=MESH
        )

    barrier = pltpu.get_barrier_semaphore()
    plane = [at(i, j) for i in range(SIDE) for j in range(SIDE) if i or j]
    peers = plane + [at_z(k) for k in range(1, DEPTH)] + [sibling]
    for peer in peers:
        pl.semaphore_signal(barrier, inc=1, device_id=peer, device_id_type=MESH)

    tok_local = pltpu.make_async_copy(tok_ref, xs.at[pl.ds(0, TOK)], loc_sem.at[0])
    tok_local.start()
    cot_local = pltpu.make_async_copy(cot_ref, cots.at[pl.ds(0, TOK)], loc_sem.at[1])
    cot_local.start()

    lane = lax.broadcasted_iota(jnp.int32, (ROWS, 128), 1)
    low = lane < 64

    def packed_mixed(core):
        g3 = wg_ref[:, MAIN : MAIN + 128].astype(F32)
        u3 = wu_ref[:, MAIN : MAIN + 128].astype(F32)
        first = jnp.where(low, g3, pltpu.roll(u3, 64, 1))
        second = jnp.where(low, pltpu.roll(g3, 64, 1), u3)
        return jnp.where(core == 0, first, second).astype(BF16)

    own_rows = pl.ds(row_of(0, 0, 0), ROWS)
    sib_rows = pl.ds(row_of(1, 0, 0), ROWS)
    own_cols = pl.ds(pl.multiple_of(c * 512, 128), MAIN)
    sib_cols = pl.ds(pl.multiple_of((1 - c) * 512, 128), MAIN)
    psib[:, 0:MAIN] = wg_ref[:, sib_cols]
    psib[:, MAIN : 2 * MAIN] = wu_ref[:, sib_cols]
    psib[:, 2 * MAIN : WIDTH] = packed_mixed(1 - c)
    wraw[own_rows, 0:MAIN] = wg_ref[:, own_cols]
    wraw[own_rows, MAIN : 2 * MAIN] = wu_ref[:, own_cols]
    wraw[own_rows, 2 * MAIN : WIDTH] = packed_mixed(c)

    am_rows = lax.broadcasted_iota(jnp.int32, (8, 128), 0)

    def largest(ref):
        return jnp.max(jnp.abs(ref[...].astype(F32)), keepdims=True)

    am_mine[0] = jnp.where(am_rows < 4, largest(wg_ref), largest(wu_ref))
    stages = [
        list(zip(plane, range(15))),
        [(sibling, 15)],
        [(at_z(k), 15 + k) for k in range(1, DEPTH)],
    ]

    def am_copies(stage):
        return [
            remote(am_mine.at[stage], am_in.at[slot], am_send.at[slot], am_recv.at[slot], device)
            for device, slot in stages[stage]
        ]

    def am_start(stage):
        for copy in am_copies(stage):
            copy.start()

    def am_finish(stage):
        best = am_mine[stage]
        for copy in am_copies(stage):
            copy.wait_recv()
        for _, slot in stages[stage]:
            best = jnp.maximum(best, am_in[slot])
        am_mine[stage + 1] = best

    pl.semaphore_wait(barrier, len(peers))
    am_start(0)

    swap = remote(psib, wraw.at[own_rows], pair_send.at[0], pair_recv.at[0], sibling)
    swap.start()

    def ag_copy(r, slot, a, b, part, axis, sign):
        rows = row_of(r, a, b)
        if part is None:
            rows, count = rows, ROWS
        else:
            rows, count = rows + part * HALF, HALF
        ref = wraw.at[pl.ds(pl.multiple_of(rows, HALF), count)]
        step = (sign % SIDE, 0) if axis == 0 else (0, sign % SIDE)
        return remote(ref, ref, ag_send.at[r, slot], ag_recv.at[r, slot], at(*place(r, *step)))

    started = []

    def ag_start(*args):
        copy = ag_copy(*args)
        copy.start()
        started.append(copy)

    def ag_wait(r, slot, a, b, part):
        ag_copy(r, slot, a, b, part, 0, 1).wait_recv()

    def first_start(r):
        ag_start(r, 1, 0, 0, None, 0, 1)
        ag_start(r, 0, 0, 0, None, 0, -1)

    def second_start(r, a):
        ag_start(r, 4 + 4 * a + 1, a, 0, None, 1, 1)
        ag_start(r, 4 + 4 * a, a, 0, None, 1, -1)

    def second_forward(r, a):
        ag_wait(r, 4 + 4 * a + 1, a, 3, None)
        ag_start(r, 4 + 4 * a + 2, a, 3, 0, 1, 1)
        ag_wait(r, 4 + 4 * a, a, 1, None)
        ag_start(r, 4 + 4 * a + 3, a, 1, 1, 1, -1)

    def second_end(r, a):
        ag_wait(r, 4 + 4 * a + 2, a, 2, 0)
        ag_wait(r, 4 + 4 * a + 3, a, 2, 1)

    first_start(0)
    second_start(0, 0)
    tok_pair = remote(tok_ref, xs.at[pl.ds(TOK, TOK)], pair_send.at[1], pair_recv.at[1], sibling)
    cot_pair = remote(cot_ref, cots.at[pl.ds(TOK, TOK)], pair_send.at[2], pair_recv.at[2], sibling)
    remote(psib, wraw.at[sib_rows], pair_send.at[0], pair_recv.at[0], sibling).wait_recv()
    first_start(1)
    second_start(1, 0)
    tok_pair.start()
    cot_pair.start()

    am_finish(0)
    am_start(1)
    am_finish(1)
    am_start(2)

    for r in (0, 1):
        ag_wait(r, 1, 3, 0, None)
        ag_start(r, 2, 3, 0, 0, 0, 1)
        ag_wait(r, 0, 1, 0, None)
        ag_start(r, 3, 1, 0, 1, 0, -1)
    for r in (0, 1):
        second_start(r, 1)
        second_start(r, 3)
    am_finish(2)

    gate_max = jnp.max(am_mine[3, 0:4, :])
    up_max = jnp.max(am_mine[3, 4:8, :])
    amax_ref[0] = gate_max
    amax_ref[1] = up_max
    col = lax.broadcasted_iota(jnp.int32, (8, WIDTH), 1)
    is_gate = (col < MAIN) | ((col >= 2 * MAIN) & (col < 2 * MAIN + 64))
    scale = 448.0 / (jnp.where(is_gate, gate_max, up_max) + 1e-06)
    scales[0] = scale
    scales[1] = 1.0 / scale

    tok_local.wait()
    cot_local.wait()
    tok_pair.wait_recv()
    cot_pair.wait_recv()

    h[...] = jnp.zeros_like(h)

    def chunk(dx, dy):
        start = pl.multiple_of(chip_at(dx, dy) * CHIP_ROWS, CHIP_ROWS)
        rows = pl.ds(start, CHIP_ROWS)
        wq[rows] = (wraw[rows].astype(F32) * scales[0, 0:1, :]).astype(BF16)

        @pl.loop(0, 2)
        def _(m):
            toks = pl.ds(pl.multiple_of(m * TOK, TOK), TOK)
            h[toks] += jnp.dot(xs[toks, rows], wq[rows], preferred_element_type=F32)

    chunk(0, 0)
    for r in (0, 1):
        second_forward(r, 0)

    @pl.loop(0, 4)
    def _(k):
        along = 1 + 2 * lax.rem(k, 2)
        chunk(along * (1 - lax.div(k, 2)), along * lax.div(k, 2))

    for r in (0, 1):
        ag_wait(r, 2, 2, 0, 0)
        ag_wait(r, 3, 2, 0, 1)
        second_start(r, 2)

    @pl.loop(0, D // 128)
    def _(b):
        cols = pl.ds(pl.multiple_of(b * 128, 128), 128)
        xt[cols, :] = xs[:, cols].T

    for a in (1, 3):
        for r in (0, 1):
            second_forward(r, a)

    @pl.loop(0, 4)
    def _(k):
        chunk(1 + 2 * lax.rem(k, 2), 1 + 2 * lax.div(k, 2))

    for r in (0, 1):
        second_end(r, 0)

    @pl.loop(0, 2)
    def _(k):
        chunk(2 * k, 2 * (1 - k))

    for r in (0, 1):
        second_forward(r, 2)
    for a in (1, 3):
        for r in (0, 1):
            second_end(r, a)

        @pl.loop(0, 2)
        def _(k):
            chunk(2 * k + a * (1 - k), 2 * (1 - k) + a * k)

    for r in (0, 1):
        second_end(r, 2)
    chunk(2, 2)

    low_tok = lax.broadcasted_iota(jnp.int32, (64, 128), 1) < 64

    def activation_grads(gate, up, cot):
        sig = jax.nn.sigmoid(gate)
        return cot * up * sig * (1.0 + gate * (1.0 - sig)), cot * gate * sig

    @pl.loop(0, 2 * TOK // 64)
    def _(m):
        toks = pl.ds(pl.multiple_of(m * 64, 64), 64)
        inv = scales[1, 0:1, :]
        hidden = h[toks] * inv
        cot = cots[toks, pl.ds(pl.multiple_of(c * 512, 128), MAIN)].astype(F32)
        dgate, dup = activation_grads(hidden[:, 0:MAIN], hidden[:, MAIN : 2 * MAIN], cot)
        mixed = hidden[:, 2 * MAIN : WIDTH]
        block = cots[toks, MAIN : MAIN + 128].astype(F32)
        block = jnp.where(c == 0, block, pltpu.roll(block, 64, 1))
        mgate, mup = activation_grads(mixed, pltpu.roll(mixed, 64, 1), block)
        both = jnp.where(low_tok, mgate, pltpu.roll(mup, 64, 1))
        for cols, part in ((slice(0, MAIN), dgate), (slice(MAIN, 2 * MAIN), dup), (slice(2 * MAIN, WIDTH), both)):
            g[toks, cols] = part.astype(BF16)
            gs[toks, cols] = (part * inv[:, cols]).astype(BF16)

    def weight_grad(r, a, b):
        return jnp.dot(xt[pl.ds(row_of(r, a, b), ROWS)], g[...], preferred_element_type=F32)

    def toward(r, axis, sign):
        return at(*place(r, *((sign % SIDE, 0) if axis == 0 else (0, sign % SIDE))))

    def s1_copy(r, a, part):
        return remote(
            s1buf.at[r, a, pl.ds(part * HALF, HALF)], s1in.at[r, a, part],
            s1_send.at[r, a, part], s1_recv.at[r, a, part], toward(r, 1, 1 - 2 * part),
        )

    def s2_copy(r, a, part):
        return remote(
            s2buf.at[r, a, part], s2in.at[r, a, part],
            s2_send.at[r, a, part], s2_recv.at[r, a, part], toward(r, 1, 1 - 2 * part),
        )

    def t1_copy(r, part):
        return remote(
            rbuf.at[r, 2, pl.ds(part * HALF, HALF)], t1in.at[r, part],
            t1_send.at[r, part], t1_recv.at[r, part], toward(r, 0, 1 - 2 * part),
        )

    def t2_copy(r, part):
        return remote(
            rbuf.at[r, 1 + 2 * part], t2in.at[r, part],
            t2_send.at[r, part], t2_recv.at[r, part], toward(r, 0, 1 - 2 * part),
        )

    for a in (2, 1, 3, 0):
        for r in (0, 1):
            s1buf[r, a] = weight_grad(r, a, 2).astype(BF16)
            s1_copy(r, a, 0).start()
            s1_copy(r, a, 1).start()

    def p_copy(dz):
        return remote(p_send.at[dz], p_in.at[dz], p_ssem.at[dz], p_rsem.at[dz], sibling)

    def input_grads(k):
        odd = lax.rem(k, 2)
        dz = odd * (4 - lax.div(k + 1, 2)) + (1 - odd) * (4 + lax.div(k, 2))
        cols = pl.ds(pl.multiple_of(lax.rem(z + dz, DEPTH) * ZCOL, ZCOL), ZCOL)
        p_send[dz] = lax.dot_general(gs[TOK:, :], wq[cols], NT, preferred_element_type=F32).astype(BF16)
        p_copy(dz).start()
        p_own[dz] = lax.dot_general(gs[:TOK, :], wq[cols], NT, preferred_element_type=F32).astype(BF16)

    def step2_piece(r, a, part):
        s1_copy(r, a, part).wait_recv()
        lo = slice(part * HALF, part * HALF + HALF)
        hi = slice((1 - part) * HALF, (1 - part) * HALF + HALF)
        grad = weight_grad(r, a, 1 + 2 * part)
        s2buf[r, a, part, lo] = (grad[lo] + s1in[r, a, part].astype(F32)).astype(BF16)
        s2buf[r, a, part, hi] = grad[hi].astype(BF16)
        s2_copy(r, a, part).start()

    def step2(a):
        for r in (0, 1):
            for part in (0, 1):
                step2_piece(r, a, part)

    def reduced(r, a):
        s2_copy(r, a, 0).wait_recv()
        s2_copy(r, a, 1).wait_recv()
        return weight_grad(r, a, 0) + s2in[r, a, 0].astype(F32) + s2in[r, a, 1].astype(F32)

    def z1_copy(part):
        return remote(
            p_own.at[4, pl.ds(part * (TOK // 2), TOK // 2)], z1in.at[part],
            z1_send.at[part], z1_recv.at[part], at_z(1 if part == 0 else DEPTH - 1),
        )

    def z_copy(step, part):
        dz = (3 - step) if part == 0 else (5 + step)
        return remote(
            p_own.at[dz], zin.at[step, part],
            z_send.at[step, part], z_recv.at[step, part], at_z(1 if part == 0 else DEPTH - 1),
        )

    def pair_sum(dz):
        p_copy(dz).wait_recv()
        return p_own[dz].astype(F32) + p_in[dz].astype(F32)

    def z_first():
        p_own[4] = pair_sum(4).astype(BF16)
        z1_copy(0).start()
        z1_copy(1).start()

    def z_round(step):
        for part in (0, 1):
            dz = (3 - step) if part == 0 else (5 + step)
            total = pair_sum(dz)
            if step == 0:
                z1_copy(part).wait_recv()
                lo = slice(part * (TOK // 2), (part + 1) * (TOK // 2))
                hi = slice((1 - part) * (TOK // 2), (2 - part) * (TOK // 2))
                p_own[dz, lo] = (total[lo] + z1in[part].astype(F32)).astype(BF16)
                p_own[dz, hi] = total[hi].astype(BF16)
            else:
                z_copy(step - 1, part).wait_recv()
                p_own[dz] = (total + zin[step - 1, part].astype(F32)).astype(BF16)
            z_copy(step, part).start()

    pl.loop(0, 4)(input_grads)
    step2(2)
    z_first()
    pl.loop(4, DEPTH)(input_grads)
    step2(1)
    step2(3)
    z_round(0)
    for r in (0, 1):
        rbuf[r, 2] = reduced(r, 2).astype(BF16)
        t1_copy(r, 0).start()
        t1_copy(r, 1).start()
    step2_piece(1, 0, 0)
    step2_piece(1, 0, 1)

    def later(r, part):
        total = reduced(r, 1 + 2 * part)
        t1_copy(r, part).wait_recv()
        lo = slice(part * HALF, part * HALF + HALF)
        hi = slice((1 - part) * HALF, (1 - part) * HALF + HALF)
        rbuf[r, 1 + 2 * part, lo] = (total[lo] + t1in[r, part].astype(F32)).astype(BF16)
        rbuf[r, 1 + 2 * part, hi] = total[hi].astype(BF16)
        t2_copy(r, part).start()

    z_round(1)
    step2_piece(0, 0, 0)
    step2_piece(0, 0, 1)
    for part in (0, 1):
        for r in (1, 0):
            later(r, part)
    z_round(2)

    def finished(r):
        total = reduced(r, 0)
        t2_copy(r, 0).wait_recv()
        t2_copy(r, 1).wait_recv()
        return (total + t2in[r, 0].astype(F32) + t2in[r, 1].astype(F32)).astype(BF16)

    final[1] = finished(1)
    last = remote(final.at[1], final_in, pair_send.at[3], pair_recv.at[3], sibling)
    last.start()
    total = pair_sum(0)
    z_copy(2, 0).wait_recv()
    z_copy(2, 1).wait_recv()
    ig_ref[...] = (total + zin[2, 0].astype(F32) + zin[2, 1].astype(F32)).astype(BF16)
    final[0] = finished(0)
    gg_ref[:, own_cols] = final[0, :, 0:MAIN]
    ug_ref[:, own_cols] = final[0, :, MAIN : 2 * MAIN]
    last.wait_recv()
    gg_ref[:, sib_cols] = final_in[:, 0:MAIN]
    ug_ref[:, sib_cols] = final_in[:, MAIN : 2 * MAIN]
    mine = final[0, :, 2 * MAIN : WIDTH].astype(F32)
    theirs = final_in[:, 2 * MAIN : WIDTH].astype(F32)
    first = jnp.where(c == 0, mine, theirs)
    second = jnp.where(c == 0, theirs, mine)
    gg_ref[:, MAIN : MAIN + 128] = jnp.where(low, first, pltpu.roll(second, 64, 1)).astype(BF16)
    ug_ref[:, MAIN : MAIN + 128] = jnp.where(low, pltpu.roll(first, 64, 1), second).astype(BF16)

    swap.wait_send()
    tok_pair.wait_send()
    cot_pair.wait_send()
    for copy in started:
        copy.wait_send()
    for stage in range(3):
        for copy in am_copies(stage):
            copy.wait_send()
    for r in (0, 1):
        for part in (0, 1):
            for a in range(SIDE):
                s1_copy(r, a, part).wait_send()
                s2_copy(r, a, part).wait_send()
            t1_copy(r, part).wait_send()
            t2_copy(r, part).wait_send()
    for dz in range(DEPTH):
        p_copy(dz).wait_send()
    for part in (0, 1):
        z1_copy(part).wait_send()
        for step in range(3):
            z_copy(step, part).wait_send()
    last.wait_send()


def hand_over(a_in, b_in, c_in, amax_in, a_out, b_out, c_out, amax_out):
    a_out[...] = a_in[...]
    b_out[...] = b_in[...]
    c_out[...] = c_in[...]
    amax_out[0] = amax_in[0]
    amax_out[1] = amax_in[1]


def on_device(tokens, cotangent, gate_weight, up_weight):
    vmem = pltpu.VMEM
    dma = pltpu.SemaphoreType.DMA
    piece = (ROWS, WIDTH)
    scratch = [
        vmem((2 * TOK, D), BF16),
        vmem((D, 2 * TOK), BF16),
        vmem((2 * TOK, WIDTH), BF16),
        vmem((D, WIDTH), BF16),
        vmem((D, WIDTH), BF16),
        vmem((2 * TOK, WIDTH), F32),
        vmem((2 * TOK, WIDTH), BF16),
        vmem((2 * TOK, WIDTH), BF16),
        vmem(piece, BF16),
        vmem((2, 8, WIDTH), F32),
        vmem((4, 8, 128), F32),
        vmem((23, 8, 128), F32),
        vmem((2, SIDE) + piece, BF16),
        vmem((2, SIDE, 2, HALF, WIDTH), BF16),
        vmem((2, SIDE, 2) + piece, BF16),
        vmem((2, SIDE, 2) + piece, BF16),
        vmem((2, SIDE) + piece, BF16),
        vmem((2, 2, HALF, WIDTH), BF16),
        vmem((2, 2) + piece, BF16),
        vmem((2,) + piece, BF16),
        vmem(piece, BF16),
        vmem((DEPTH, TOK, ZCOL), BF16),
        vmem((DEPTH, TOK, ZCOL), BF16),
        vmem((DEPTH, TOK, ZCOL), BF16),
        vmem((2, TOK // 2, ZCOL), BF16),
        vmem((3, 2, TOK, ZCOL), BF16),
        dma((2,)), dma((4,)), dma((4,)), dma((2, 20)), dma((2, 20)), dma((23,)), dma((23,)),
        dma((2, SIDE, 2)), dma((2, SIDE, 2)), dma((2, SIDE, 2)), dma((2, SIDE, 2)),
        dma((2, 2)), dma((2, 2)), dma((2, 2)), dma((2, 2)),
        dma((DEPTH,)), dma((DEPTH,)), dma((2,)), dma((2,)), dma((3, 2)), dma((3, 2)),
    ]
    whole = pl.BlockSpec(memory_space=pltpu.VMEM)
    outs = pl.pallas_call(
        kernel,
        out_shape=(
            jax.ShapeDtypeStruct((TOK, ZCOL), BF16),
            jax.ShapeDtypeStruct((ROWS, WIDTH), BF16),
            jax.ShapeDtypeStruct((ROWS, WIDTH), BF16),
            jax.ShapeDtypeStruct((2,), F32),
        ),
        in_specs=[pl.BlockSpec(memory_space=pl.ANY)] * 2 + [whole] * 2,
        out_specs=(whole, whole, whole, pl.BlockSpec(memory_space=pltpu.SMEM)),
        scratch_shapes=scratch,
        compiler_params=pltpu.CompilerParams(
            collective_id=0, has_side_effects=True, vmem_limit_bytes=62 * 1024 * 1024
        ),
        cost_estimate=pl.CostEstimate(flops=3 * 2 * 512 * 4096 * 896, bytes_accessed=4 << 20, transcendentals=512 * 448),
        name="swiglu_backward",
    )(tokens, cotangent, gate_weight, up_weight)
    scalars = pl.BlockSpec(memory_space=pltpu.SMEM)
    return pl.pallas_call(
        hand_over,
        out_shape=tuple(jax.ShapeDtypeStruct(o.shape, o.dtype) for o in outs),
        in_specs=[whole] * 3 + [scalars],
        out_specs=(whole,) * 3 + (scalars,),
        compiler_params=pltpu.CompilerParams(vmem_limit_bytes=62 * 1024 * 1024),
        name="hand_over",
    )(*outs)


def solution(mesh):
    in_specs = (P("fsdp", None), P("fsdp", "tp"), P("fsdp", "tp"), P("fsdp", "tp"))
    out_specs = (P("fsdp", "tp"), P("fsdp", "tp"), P("fsdp", "tp"), P())
    return jax.shard_map(
        on_device, mesh=mesh, in_specs=in_specs, out_specs=out_specs, check_vma=False
    )
```

```python
import jax
import jax.numpy as jnp
from jax import lax
from jax.experimental import pallas as pl
from jax.experimental.pallas import tpu as pltpu
from jax.sharding import PartitionSpec as P

MESH = pl.DeviceIdType.MESH
F32 = jnp.float32
BF16 = jnp.bfloat16
SIDE = 4
DEPTH = 8
ROWS = 128
HALF = ROWS // 2
CHIP_ROWS = 2 * ROWS
TOK = 256
D = 4096
WIDTH = 896
MAIN = 384
GROUPS = ((0, 512), (512, 384))
ZCOL = D // DEPTH
NT = (((1,), (1,)), ((), ()))


def kernel(
    tok_ref, cot_ref, wg_hbm, wu_hbm,
    ig_hbm, gg_hbm, ug_hbm, amax_ref,
    wg_ref, wu_ref, ig_ref, gg_ref, ug_ref,
    xs, xt, cots, wraw, wq, h, g, gs, psib, scales, am_mine, am_in,
    s1buf, s1in, s2buf, s2in, rbuf, t1in, t2in, final, final_in,
    p_own, p_send, p_in, z1in, zin,
    loc_sem, pair_send, pair_recv, ag_send, ag_recv, am_send, am_recv,
    s1_send, s1_recv, s2_send, s2_recv, t1_send, t1_recv, t2_send, t2_recv,
    p_ssem, p_rsem, z1_send, z1_recv, z_send, z_recv,
):
    f = lax.axis_index("fsdp")
    z = lax.axis_index("tp")
    c = lax.rem(f, 2)
    chip = lax.div(f, 2)
    x = lax.div(chip, SIDE)
    y = lax.rem(chip, SIDE)

    def chip_at(dx, dy):
        return lax.rem(x + dx, SIDE) * SIDE + lax.rem(y + dy, SIDE)

    def at(dx, dy):
        return (chip_at(dx, dy) * 2 + c, z)

    def at_z(dz):
        return (f, lax.rem(z + dz, DEPTH))

    sibling = (chip * 2 + 1 - c, z)

    def place(r, a, b):
        return (a, b) if r == 0 else (b, a)

    def row_of(r, a, b):
        return pl.multiple_of(chip_at(*place(r, a, b)) * CHIP_ROWS + (c if r == 0 else 1 - c) * ROWS, ROWS)

    def remote(src, dst, ssem, rsem, device):
        return pltpu.make_async_remote_copy(
            src_ref=src, dst_ref=dst, send_sem=ssem, recv_sem=rsem, device_id=device, device_id_type=MESH
        )

    barrier = pltpu.get_barrier_semaphore()
    plane = [at(i, j) for i in range(SIDE) for j in range(SIDE) if i or j]
    peers = plane + [at_z(k) for k in range(1, DEPTH)] + [sibling]
    for peer in peers:
        pl.semaphore_signal(barrier, inc=1, device_id=peer, device_id_type=MESH)

    w_local = [
        pltpu.make_async_copy(wg_hbm, wg_ref, loc_sem.at[2]),
        pltpu.make_async_copy(wu_hbm, wu_ref, loc_sem.at[3]),
    ]
    for copy in w_local:
        copy.start()
    tok_local = pltpu.make_async_copy(tok_ref, xs.at[pl.ds(0, TOK)], loc_sem.at[0])
    tok_local.start()
    cot_local = pltpu.make_async_copy(cot_ref, cots.at[pl.ds(0, TOK)], loc_sem.at[1])
    cot_local.start()

    lane = lax.broadcasted_iota(jnp.int32, (ROWS, 128), 1)
    low = lane < 64

    def packed_mixed(core):
        g3 = wg_ref[:, MAIN : MAIN + 128].astype(F32)
        u3 = wu_ref[:, MAIN : MAIN + 128].astype(F32)
        first = jnp.where(low, g3, pltpu.roll(u3, 64, 1))
        second = jnp.where(low, pltpu.roll(g3, 64, 1), u3)
        return jnp.where(core == 0, first, second).astype(BF16)

    for copy in w_local:
        copy.wait()
    own_rows = pl.ds(row_of(0, 0, 0), ROWS)
    sib_rows = pl.ds(row_of(1, 0, 0), ROWS)

    def packed(out, rows, first, core):
        cols = pl.ds(first, 256)
        out[0][rows, 0:256] = wg_ref[:, cols]
        out[0][rows, 256:512] = wu_ref[:, cols]
        cols = pl.ds(pl.multiple_of(first + 256, 128), 128)
        out[1][rows, 0:128] = wg_ref[:, cols]
        out[1][rows, 128:256] = wu_ref[:, cols]
        out[1][rows, 256:384] = packed_mixed(core)

    own_first = pl.multiple_of(c * 512, 128)
    sib_first = pl.multiple_of((1 - c) * 512, 128)
    packed(psib, slice(0, ROWS), sib_first, 1 - c)
    packed(wraw, own_rows, own_first, c)

    am_rows = lax.broadcasted_iota(jnp.int32, (8, 128), 0)

    def largest(ref):
        return jnp.max(jnp.abs(ref[...].astype(F32)), keepdims=True)

    am_mine[0] = jnp.where(am_rows < 4, largest(wg_ref), largest(wu_ref))
    stages = [
        list(zip(plane, range(15))),
        [(sibling, 15)],
        [(at_z(k), 15 + k) for k in range(1, DEPTH)],
    ]

    def am_copies(stage):
        return [
            remote(am_mine.at[stage], am_in.at[slot], am_send.at[slot], am_recv.at[slot], device)
            for device, slot in stages[stage]
        ]

    def am_start(stage):
        for copy in am_copies(stage):
            copy.start()

    def am_finish(stage):
        best = am_mine[stage]
        for copy in am_copies(stage):
            copy.wait_recv()
        for _, slot in stages[stage]:
            best = jnp.maximum(best, am_in[slot])
        am_mine[stage + 1] = best

    pl.semaphore_wait(barrier, len(peers))

    def swap_copy(q, rows):
        return remote(psib[q], wraw[q].at[rows], pair_send.at[q], pair_recv.at[q], sibling)

    for q in (0, 1):
        swap_copy(q, own_rows).start()

    def ag_copy(q, r, slot, a, b, part, axis, sign):
        rows = row_of(r, a, b)
        if part is None:
            rows, count = rows, ROWS
        else:
            rows, count = rows + part * HALF, HALF
        ref = wraw[q].at[pl.ds(pl.multiple_of(rows, HALF), count)]
        step = (sign % SIDE, 0) if axis == 0 else (0, sign % SIDE)
        return remote(ref, ref, ag_send.at[q, r, slot], ag_recv.at[q, r, slot], at(*place(r, *step)))

    started = []

    def ag_start(*args):
        copy = ag_copy(*args)
        copy.start()
        started.append(copy)

    def ag_wait(q, r, slot, a, b, part):
        ag_copy(q, r, slot, a, b, part, 0, 1).wait_recv()

    def first_start(q, r):
        ag_start(q, r, 1, 0, 0, None, 0, 1)
        ag_start(q, r, 0, 0, 0, None, 0, -1)

    def first_forward(q):
        for r in (0, 1):
            ag_wait(q, r, 1, 3, 0, None)
            ag_start(q, r, 2, 3, 0, 0, 0, 1)
            ag_wait(q, r, 0, 1, 0, None)
            ag_start(q, r, 3, 1, 0, 1, 0, -1)
            second_start(q, r, 1)
            second_start(q, r, 3)

    def first_end(q):
        for r in (0, 1):
            ag_wait(q, r, 2, 2, 0, 0)
            ag_wait(q, r, 3, 2, 0, 1)
            second_start(q, r, 2)

    def second_start(q, r, a):
        ag_start(q, r, 4 + 4 * a + 1, a, 0, None, 1, 1)
        ag_start(q, r, 4 + 4 * a, a, 0, None, 1, -1)

    def second_forward(q, a):
        for r in (0, 1):
            ag_wait(q, r, 4 + 4 * a + 1, a, 3, None)
            ag_start(q, r, 4 + 4 * a + 2, a, 3, 0, 1, 1)
            ag_wait(q, r, 4 + 4 * a, a, 1, None)
            ag_start(q, r, 4 + 4 * a + 3, a, 1, 1, 1, -1)

    def second_end(q, a):
        for r in (0, 1):
            ag_wait(q, r, 4 + 4 * a + 2, a, 2, 0)
            ag_wait(q, r, 4 + 4 * a + 3, a, 2, 1)

    first_start(0, 0)
    second_start(0, 0, 0)
    tok_pair = remote(tok_ref, xs.at[pl.ds(TOK, TOK)], pair_send.at[2], pair_recv.at[2], sibling)
    cot_pair = remote(cot_ref, cots.at[pl.ds(TOK, TOK)], pair_send.at[3], pair_recv.at[3], sibling)
    swap_copy(0, sib_rows).wait_recv()
    first_start(0, 1)
    second_start(0, 1, 0)
    am_start(0)
    tok_pair.start()
    cot_pair.start()
    first_forward(0)

    tok_local.wait()
    tok_pair.wait_recv()

    @pl.loop(0, D // 128)
    def _(b):
        cols = pl.ds(pl.multiple_of(b * 128, 128), 128)
        xt[cols, :] = xs[:, cols].T

    am_finish(0)
    am_start(1)
    second_forward(0, 0)
    am_finish(1)
    am_start(2)
    first_end(0)
    swap_copy(1, sib_rows).wait_recv()
    for r in (0, 1):
        first_start(1, r)
        second_start(1, r, 0)
    am_finish(2)

    gate_max = jnp.max(am_mine[3, 0:4, :])
    up_max = jnp.max(am_mine[3, 4:8, :])
    amax_ref[0] = gate_max
    amax_ref[1] = up_max
    col = lax.broadcasted_iota(jnp.int32, (8, WIDTH), 1)
    is_gate = (col < 256) | ((col >= 512) & (col < 640)) | ((col >= 768) & (col < 832))
    scale = 448.0 / (jnp.where(is_gate, gate_max, up_max) + 1e-06)
    scales[0] = scale
    scales[1] = 1.0 / scale

    cot_local.wait()
    cot_pair.wait_recv()

    h[...] = jnp.zeros_like(h)

    def chunk(q, dx, dy):
        start = pl.multiple_of(chip_at(dx, dy) * CHIP_ROWS, CHIP_ROWS)
        rows = pl.ds(start, CHIP_ROWS)
        group = slice(GROUPS[q][0], sum(GROUPS[q]))
        wq[rows, group] = (wraw[q][rows].astype(F32) * scales[0, 0:1, group]).astype(BF16)

        @pl.loop(0, 2)
        def _(m):
            toks = pl.ds(pl.multiple_of(m * TOK, TOK), TOK)
            h[toks, group] += jnp.dot(xs[toks, rows], wq[rows, group], preferred_element_type=F32)

    def chunks_near(q):
        @pl.loop(0, 5)
        def _(k):
            along = jnp.where(k == 4, 0, 1 + 2 * lax.rem(k, 2))
            flip = lax.rem(lax.div(k, 2), 2)
            chunk(q, along * (1 - flip), along * flip)

    def chunks_corner(q):
        @pl.loop(0, 4)
        def _(k):
            chunk(q, 1 + 2 * lax.rem(k, 2), 1 + 2 * lax.div(k, 2))

    def chunks_across(q, a):
        @pl.loop(0, 2)
        def _(k):
            chunk(q, 2 * k + a * (1 - k), 2 * (1 - k) + a * k)

    low_tok = lax.broadcasted_iota(jnp.int32, (64, 128), 1) < 64

    def activation_grads(gate, up, cot):
        sig = jax.nn.sigmoid(gate)
        return cot * up * sig * (1.0 + gate * (1.0 - sig)), cot * gate * sig

    def hidden_grads(q):
        @pl.loop(0, 2 * TOK // 64)
        def _(m):
            toks = pl.ds(pl.multiple_of(m * 64, 64), 64)
            start, width = GROUPS[q]
            inv = scales[1, 0:1, start : start + width]
            hidden = h[toks, start : start + width] * inv
            main = 256 if q == 0 else 128
            cot = cots[toks, pl.ds(pl.multiple_of(c * 512 + 256 * q, 128), main)].astype(F32)
            dgate, dup = activation_grads(hidden[:, 0:main], hidden[:, main : 2 * main], cot)
            parts = [(0, main, dgate), (main, 2 * main, dup)]
            if q == 1:
                mixed = hidden[:, 256:384]
                block = cots[toks, MAIN : MAIN + 128].astype(F32)
                block = jnp.where(c == 0, block, pltpu.roll(block, 64, 1))
                mgate, mup = activation_grads(mixed, pltpu.roll(mixed, 64, 1), block)
                parts.append((256, 384, jnp.where(low_tok, mgate, pltpu.roll(mup, 64, 1))))
            for lo, hi, part in parts:
                g[toks, start + lo : start + hi] = part.astype(BF16)
                gs[toks, start + lo : start + hi] = (part * inv[:, lo:hi]).astype(BF16)

    def weight_grad(q, r, a, b):
        group = slice(GROUPS[q][0], sum(GROUPS[q]))
        return jnp.dot(xt[pl.ds(row_of(r, a, b), ROWS)], g[:, group], preferred_element_type=F32)

    def toward(r, axis, sign):
        return at(*place(r, *((sign % SIDE, 0) if axis == 0 else (0, sign % SIDE))))

    def s1_copy(q, r, a, part):
        return remote(
            s1buf[q].at[r, a, pl.ds(part * HALF, HALF)], s1in[q].at[r, a, part],
            s1_send.at[q, r, a, part], s1_recv.at[q, r, a, part], toward(r, 1, 1 - 2 * part),
        )

    def s2_copy(q, r, a, part):
        return remote(
            s2buf[q].at[r, a, part], s2in[q].at[r, a, part],
            s2_send.at[q, r, a, part], s2_recv.at[q, r, a, part], toward(r, 1, 1 - 2 * part),
        )

    def t1_copy(q, r, part):
        return remote(
            rbuf[q].at[r, 2, pl.ds(part * HALF, HALF)], t1in[q].at[r, part],
            t1_send.at[q, r, part], t1_recv.at[q, r, part], toward(r, 0, 1 - 2 * part),
        )

    def t2_copy(q, r, part):
        return remote(
            rbuf[q].at[r, 1 + 2 * part], t2in[q].at[r, part],
            t2_send.at[q, r, part], t2_recv.at[q, r, part], toward(r, 0, 1 - 2 * part),
        )

    def step1(q):
        for a in (2, 1, 3, 0):
            for r in (0, 1):
                s1buf[q][r, a] = weight_grad(q, r, a, 2).astype(BF16)
                s1_copy(q, r, a, 0).start()
                s1_copy(q, r, a, 1).start()

    chunks_near(0)
    second_forward(0, 1)
    second_forward(0, 3)
    chunks_corner(0)
    second_end(0, 0)
    second_forward(0, 2)
    chunks_across(0, 0)
    first_forward(1)
    second_forward(1, 0)
    chunks_near(1)
    for a in (1, 3):
        second_end(0, a)
        chunks_across(0, a)
    first_end(1)
    second_end(0, 2)
    chunk(0, 2, 2)
    hidden_grads(0)
    second_forward(1, 1)
    second_forward(1, 3)
    chunks_corner(1)
    second_end(1, 0)
    chunks_across(1, 0)
    second_forward(1, 2)
    step1(0)
    for a in (1, 3):
        second_end(1, a)
        chunks_across(1, a)
    second_end(1, 2)
    chunk(1, 2, 2)
    hidden_grads(1)
    step1(1)

    def p_copy(dz):
        return remote(p_send.at[dz], p_in.at[dz], p_ssem.at[dz], p_rsem.at[dz], sibling)

    def input_grads(k):
        odd = lax.rem(k, 2)
        dz = odd * (4 - lax.div(k + 1, 2)) + (1 - odd) * (4 + lax.div(k, 2))
        cols = pl.ds(pl.multiple_of(lax.rem(z + dz, DEPTH) * ZCOL, ZCOL), ZCOL)
        p_send[dz] = lax.dot_general(gs[TOK:, :], wq[cols], NT, preferred_element_type=F32).astype(BF16)
        p_copy(dz).start()
        p_own[dz] = lax.dot_general(gs[:TOK, :], wq[cols], NT, preferred_element_type=F32).astype(BF16)

    def added(out, total, part, extra):
        lo = slice(part * HALF, part * HALF + HALF)
        hi = slice((1 - part) * HALF, (1 - part) * HALF + HALF)
        out[lo] = (total[lo] + extra.astype(F32)).astype(BF16)
        out[hi] = total[hi].astype(BF16)

    def step2(a, halves=(0, 1), groups=(0, 1)):
        for q in groups:
            for r in halves:
                for part in (0, 1):
                    s1_copy(q, r, a, part).wait_recv()
                    grad = weight_grad(q, r, a, 1 + 2 * part)
                    added(s2buf[q].at[r, a, part], grad, part, s1in[q][r, a, part])
                    s2_copy(q, r, a, part).start()

    def reduced(q, r, a):
        s2_copy(q, r, a, 0).wait_recv()
        s2_copy(q, r, a, 1).wait_recv()
        return weight_grad(q, r, a, 0) + s2in[q][r, a, 0].astype(F32) + s2in[q][r, a, 1].astype(F32)

    def z1_copy(part):
        return remote(
            p_own.at[4, pl.ds(part * (TOK // 2), TOK // 2)], z1in.at[part],
            z1_send.at[part], z1_recv.at[part], at_z(1 if part == 0 else DEPTH - 1),
        )

    def z_copy(step, part):
        dz = (3 - step) if part == 0 else (5 + step)
        return remote(
            p_own.at[dz], zin.at[step, part],
            z_send.at[step, part], z_recv.at[step, part], at_z(1 if part == 0 else DEPTH - 1),
        )

    def pair_sum(dz):
        p_copy(dz).wait_recv()
        return p_own[dz].astype(F32) + p_in[dz].astype(F32)

    def z_first():
        p_own[4] = pair_sum(4).astype(BF16)
        z1_copy(0).start()
        z1_copy(1).start()

    def z_round(step):
        for part in (0, 1):
            dz = (3 - step) if part == 0 else (5 + step)
            total = pair_sum(dz)
            if step == 0:
                z1_copy(part).wait_recv()
                lo = slice(part * (TOK // 2), (part + 1) * (TOK // 2))
                hi = slice((1 - part) * (TOK // 2), (2 - part) * (TOK // 2))
                p_own[dz, lo] = (total[lo] + z1in[part].astype(F32)).astype(BF16)
                p_own[dz, hi] = total[hi].astype(BF16)
            else:
                z_copy(step - 1, part).wait_recv()
                p_own[dz] = (total + zin[step - 1, part].astype(F32)).astype(BF16)
            z_copy(step, part).start()

    def reduced_across(q):
        for r in (0, 1):
            rbuf[q][r, 2] = reduced(q, r, 2).astype(BF16)
            t1_copy(q, r, 0).start()
            t1_copy(q, r, 1).start()

    def later(q, r, part):
        total = reduced(q, r, 1 + 2 * part)
        t1_copy(q, r, part).wait_recv()
        added(rbuf[q].at[r, 1 + 2 * part], total, part, t1in[q][r, part])
        t2_copy(q, r, part).start()

    pl.loop(0, 3)(input_grads)
    z_first()
    step2(2)
    pl.loop(3, 5)(input_grads)
    z_round(0)
    step2(1)
    pl.loop(5, DEPTH)(input_grads)
    reduced_across(0)
    reduced_across(1)
    step2(3)
    z_round(1)
    step2(0, (1,))
    step2(0, (0,), (0,))
    for part in (0, 1):
        for q in (0, 1):
            later(q, 1, part)
    z_round(2)
    step2(0, (0,), (1,))
    for part in (0, 1):
        for q in (0, 1):
            later(q, 0, part)

    def finished(q, r):
        total = reduced(q, r, 0)
        t2_copy(q, r, 0).wait_recv()
        t2_copy(q, r, 1).wait_recv()
        return (total + t2in[q][r, 0].astype(F32) + t2in[q][r, 1].astype(F32)).astype(BF16)

    def last_copy(q):
        return remote(final[q].at[1], final_in[q], pair_send.at[4 + q], pair_recv.at[4 + q], sibling)

    for q in (0, 1):
        final[q][1] = finished(q, 1)
        last_copy(q).start()
    total = pair_sum(0)
    z_copy(2, 0).wait_recv()
    z_copy(2, 1).wait_recv()
    ig_ref[...] = (total + zin[2, 0].astype(F32) + zin[2, 1].astype(F32)).astype(BF16)
    ig_out = pltpu.make_async_copy(ig_ref, ig_hbm, loc_sem.at[4])
    ig_out.start()
    for q in (0, 1):
        final[q][0] = finished(q, 0)

    def placed(ref, first):
        cols = pl.ds(first, 256)
        gg_ref[:, cols] = ref[0][:, 0:256]
        ug_ref[:, cols] = ref[0][:, 256:512]
        cols = pl.ds(pl.multiple_of(first + 256, 128), 128)
        gg_ref[:, cols] = ref[1][:, 0:128]
        ug_ref[:, cols] = ref[1][:, 128:256]
        return ref[1][:, 256:384].astype(F32)

    mine = placed([final[q].at[0] for q in (0, 1)], own_first)
    for q in (0, 1):
        last_copy(q).wait_recv()
    theirs = placed(final_in, sib_first)
    first = jnp.where(c == 0, mine, theirs)
    second = jnp.where(c == 0, theirs, mine)
    gg_ref[:, MAIN : MAIN + 128] = jnp.where(low, first, pltpu.roll(second, 64, 1)).astype(BF16)
    ug_ref[:, MAIN : MAIN + 128] = jnp.where(low, pltpu.roll(first, 64, 1), second).astype(BF16)

    outs = [
        ig_out,
        pltpu.make_async_copy(gg_ref, gg_hbm, loc_sem.at[5]),
        pltpu.make_async_copy(ug_ref, ug_hbm, loc_sem.at[6]),
    ]
    outs[1].start()
    outs[2].start()

    for q in (0, 1):
        swap_copy(q, own_rows).wait_send()
        last_copy(q).wait_send()
    tok_pair.wait_send()
    cot_pair.wait_send()
    for copy in started:
        copy.wait_send()
    for stage in range(3):
        for copy in am_copies(stage):
            copy.wait_send()
    for q in (0, 1):
        for r in (0, 1):
            for part in (0, 1):
                for a in range(SIDE):
                    s1_copy(q, r, a, part).wait_send()
                    s2_copy(q, r, a, part).wait_send()
                t1_copy(q, r, part).wait_send()
                t2_copy(q, r, part).wait_send()
    for dz in range(DEPTH):
        p_copy(dz).wait_send()
    for part in (0, 1):
        z1_copy(part).wait_send()
        for step in range(3):
            z_copy(step, part).wait_send()
    for copy in outs:
        copy.wait()


def hand_over(a_in, b_in, c_in, amax_in, a_out, b_out, c_out, amax_out):
    a_out[...] = a_in[...]
    b_out[...] = b_in[...]
    c_out[...] = c_in[...]
    amax_out[0] = amax_in[0]
    amax_out[1] = amax_in[1]


def on_device(tokens, cotangent, gate_weight, up_weight):
    vmem = pltpu.VMEM
    dma = pltpu.SemaphoreType.DMA

    def both(*shape):
        return tuple(vmem(shape + (width,), BF16) for _, width in GROUPS)

    scratch = [
        vmem((ROWS, WIDTH), BF16),
        vmem((ROWS, WIDTH), BF16),
        vmem((TOK, ZCOL), BF16),
        vmem((ROWS, WIDTH), BF16),
        vmem((ROWS, WIDTH), BF16),
        vmem((2 * TOK, D), BF16),
        vmem((D, 2 * TOK), BF16),
        vmem((2 * TOK, WIDTH), BF16),
        both(D),
        vmem((D, WIDTH), BF16),
        vmem((2 * TOK, WIDTH), F32),
        vmem((2 * TOK, WIDTH), BF16),
        vmem((2 * TOK, WIDTH), BF16),
        both(ROWS),
        vmem((2, 8, WIDTH), F32),
        vmem((4, 8, 128), F32),
        vmem((23, 8, 128), F32),
        both(2, SIDE, ROWS),
        both(2, SIDE, 2, HALF),
        both(2, SIDE, 2, ROWS),
        both(2, SIDE, 2, ROWS),
        both(2, SIDE, ROWS),
        both(2, 2, HALF),
        both(2, 2, ROWS),
        both(2, ROWS),
        both(ROWS),
        vmem((DEPTH, TOK, ZCOL), BF16),
        vmem((DEPTH, TOK, ZCOL), BF16),
        vmem((DEPTH, TOK, ZCOL), BF16),
        vmem((2, TOK // 2, ZCOL), BF16),
        vmem((3, 2, TOK, ZCOL), BF16),
        dma((7,)), dma((6,)), dma((6,)), dma((2, 2, 20)), dma((2, 2, 20)), dma((23,)), dma((23,)),
        dma((2, 2, SIDE, 2)), dma((2, 2, SIDE, 2)), dma((2, 2, SIDE, 2)), dma((2, 2, SIDE, 2)),
        dma((2, 2, 2)), dma((2, 2, 2)), dma((2, 2, 2)), dma((2, 2, 2)),
        dma((DEPTH,)), dma((DEPTH,)), dma((2,)), dma((2,)), dma((3, 2)), dma((3, 2)),
    ]
    anywhere = pl.BlockSpec(memory_space=pl.ANY)
    scalars = pl.BlockSpec(memory_space=pltpu.SMEM)
    whole = pl.BlockSpec(memory_space=pltpu.VMEM)
    outs = pl.pallas_call(
        kernel,
        out_shape=(
            jax.ShapeDtypeStruct((TOK, ZCOL), BF16),
            jax.ShapeDtypeStruct((ROWS, WIDTH), BF16),
            jax.ShapeDtypeStruct((ROWS, WIDTH), BF16),
            jax.ShapeDtypeStruct((2,), F32),
        ),
        in_specs=[anywhere] * 4,
        out_specs=(anywhere,) * 3 + (scalars,),
        scratch_shapes=scratch,
        compiler_params=pltpu.CompilerParams(
            collective_id=0, has_side_effects=True, vmem_limit_bytes=62 * 1024 * 1024
        ),
        cost_estimate=pl.CostEstimate(flops=3 * 2 * 512 * 4096 * 896, bytes_accessed=4 << 20, transcendentals=512 * 448),
        name="swiglu_backward",
    )(tokens, cotangent, gate_weight, up_weight)
    return pl.pallas_call(
        hand_over,
        out_shape=tuple(jax.ShapeDtypeStruct(o.shape, o.dtype) for o in outs),
        in_specs=[whole] * 3 + [scalars],
        out_specs=(whole,) * 3 + (scalars,),
        compiler_params=pltpu.CompilerParams(vmem_limit_bytes=62 * 1024 * 1024),
        name="hand_over",
    )(*outs)


def solution(mesh):
    in_specs = (P("fsdp", None), P("fsdp", "tp"), P("fsdp", "tp"), P("fsdp", "tp"))
    out_specs = (P("fsdp", "tp"), P("fsdp", "tp"), P("fsdp", "tp"), P())
    return jax.shard_map(
        on_device, mesh=mesh, in_specs=in_specs, out_specs=out_specs, check_vma=False
    )
```

```python
import jax
import jax.numpy as jnp
from jax import lax
from jax.experimental import pallas as pl
from jax.experimental.pallas import tpu as pltpu
from jax.sharding import PartitionSpec as P

MESH = pl.DeviceIdType.MESH
F32 = jnp.float32
BF16 = jnp.bfloat16
SIDE = 4
DEPTH = 8
ROWS = 128
HALF = ROWS // 2
CHIP_ROWS = 2 * ROWS
TOK = 256
D = 4096
WIDTH = 896
MAIN = 384
GROUPS = ((0, 512), (512, 384))
ZCOL = D // DEPTH
NT = (((1,), (1,)), ((), ()))


def kernel(
    tok_ref, cot_ref, wg_hbm, wu_hbm,
    ig_hbm, gg_hbm, ug_hbm, amax_ref,
    wg_ref, wu_ref, ig_ref, gg_ref, ug_ref,
    xs, xt, cots, wraw, wq, h, g, gs, psib, scales, am_mine, am_in,
    s1buf, s1in, s2buf, s2in, rbuf, t1in, t2in, final, final_in,
    p_own, p_send, p_in, z1in, zin,
    loc_sem, pair_send, pair_recv, ag_send, ag_recv, am_send, am_recv,
    s1_send, s1_recv, s2_send, s2_recv, t1_send, t1_recv, t2_send, t2_recv,
    p_ssem, p_rsem, z1_send, z1_recv, z_send, z_recv,
):
    f = lax.axis_index("fsdp")
    z = lax.axis_index("tp")
    c = lax.rem(f, 2)
    chip = lax.div(f, 2)
    x = lax.div(chip, SIDE)
    y = lax.rem(chip, SIDE)

    def chip_at(dx, dy):
        return lax.rem(x + dx, SIDE) * SIDE + lax.rem(y + dy, SIDE)

    def at(dx, dy):
        return (chip_at(dx, dy) * 2 + c, z)

    def at_z(dz):
        return (f, lax.rem(z + dz, DEPTH))

    sibling = (chip * 2 + 1 - c, z)

    def place(r, a, b):
        return (a, b) if r == 0 else (b, a)

    def row_of(r, a, b):
        return pl.multiple_of(chip_at(*place(r, a, b)) * CHIP_ROWS + (c if r == 0 else 1 - c) * ROWS, ROWS)

    def remote(src, dst, ssem, rsem, device):
        return pltpu.make_async_remote_copy(
            src_ref=src, dst_ref=dst, send_sem=ssem, recv_sem=rsem, device_id=device, device_id_type=MESH
        )

    barrier = pltpu.get_barrier_semaphore()
    x_peers = [at(k, 0) for k in range(1, SIDE)]
    y_peers = [at(0, k) for k in range(1, SIDE)]
    z_peers = [at_z(k) for k in range(1, DEPTH)]
    peers = x_peers + y_peers + z_peers + [sibling]
    for peer in peers:
        pl.semaphore_signal(barrier, inc=1, device_id=peer, device_id_type=MESH)

    w_local = [
        pltpu.make_async_copy(wg_hbm, wg_ref, loc_sem.at[2]),
        pltpu.make_async_copy(wu_hbm, wu_ref, loc_sem.at[3]),
    ]
    for copy in w_local:
        copy.start()
    tok_local = pltpu.make_async_copy(tok_ref, xs.at[pl.ds(0, TOK)], loc_sem.at[0])
    tok_local.start()
    cot_local = pltpu.make_async_copy(cot_ref, cots.at[pl.ds(0, TOK)], loc_sem.at[1])
    cot_local.start()

    lane = lax.broadcasted_iota(jnp.int32, (ROWS, 128), 1)
    low = lane < 64

    def packed_mixed(core):
        g3 = wg_ref[:, MAIN : MAIN + 128].astype(F32)
        u3 = wu_ref[:, MAIN : MAIN + 128].astype(F32)
        first = jnp.where(low, g3, pltpu.roll(u3, 64, 1))
        second = jnp.where(low, pltpu.roll(g3, 64, 1), u3)
        return jnp.where(core == 0, first, second).astype(BF16)

    for copy in w_local:
        copy.wait()
    own_rows = pl.ds(row_of(0, 0, 0), ROWS)
    sib_rows = pl.ds(row_of(1, 0, 0), ROWS)

    def packed(out, rows, first, core):
        cols = pl.ds(first, 256)
        out[0][rows, 0:256] = wg_ref[:, cols]
        out[0][rows, 256:512] = wu_ref[:, cols]
        cols = pl.ds(pl.multiple_of(first + 256, 128), 128)
        out[1][rows, 0:128] = wg_ref[:, cols]
        out[1][rows, 128:256] = wu_ref[:, cols]
        out[1][rows, 256:384] = packed_mixed(core)

    own_first = pl.multiple_of(c * 512, 128)
    sib_first = pl.multiple_of((1 - c) * 512, 128)
    packed(psib, slice(0, ROWS), sib_first, 1 - c)
    packed(wraw, own_rows, own_first, c)

    am_rows = lax.broadcasted_iota(jnp.int32, (8, 128), 0)

    def largest(ref):
        return jnp.max(jnp.abs(ref[...].astype(F32)), keepdims=True)

    am_mine[0] = jnp.where(am_rows < 4, largest(wg_ref), largest(wu_ref))
    stages = [x_peers, y_peers, [sibling], z_peers]
    slots, used = [], 0
    for devices in stages:
        slots.append(range(used, used + len(devices)))
        used += len(devices)

    def am_copies(stage):
        return [
            remote(am_mine.at[stage], am_in.at[slot], am_send.at[slot], am_recv.at[slot], device)
            for device, slot in zip(stages[stage], slots[stage])
        ]

    def am_start(stage):
        for copy in am_copies(stage):
            copy.start()

    def am_finish(stage):
        best = am_mine[stage]
        for copy in am_copies(stage):
            copy.wait_recv()
        for slot in slots[stage]:
            best = jnp.maximum(best, am_in[slot])
        am_mine[stage + 1] = best

    pl.semaphore_wait(barrier, len(peers))

    def swap_copy(q, rows):
        return remote(psib[q], wraw[q].at[rows], pair_send.at[q], pair_recv.at[q], sibling)

    for q in (0, 1):
        swap_copy(q, own_rows).start()

    def ag_copy(q, r, slot, a, b, part, axis, sign):
        rows = row_of(r, a, b)
        if part is None:
            rows, count = rows, ROWS
        else:
            rows, count = rows + part * HALF, HALF
        ref = wraw[q].at[pl.ds(pl.multiple_of(rows, HALF), count)]
        step = (sign % SIDE, 0) if axis == 0 else (0, sign % SIDE)
        return remote(ref, ref, ag_send.at[q, r, slot], ag_recv.at[q, r, slot], at(*place(r, *step)))

    started = []

    def ag_start(*args):
        copy = ag_copy(*args)
        copy.start()
        started.append(copy)

    def ag_wait(q, r, slot, a, b, part):
        ag_copy(q, r, slot, a, b, part, 0, 1).wait_recv()

    def first_start(q, r):
        ag_start(q, r, 1, 0, 0, None, 0, 1)
        ag_start(q, r, 0, 0, 0, None, 0, -1)

    def first_forward(q):
        for r in (0, 1):
            ag_wait(q, r, 1, 3, 0, None)
            ag_start(q, r, 2, 3, 0, 0, 0, 1)
            ag_wait(q, r, 0, 1, 0, None)
            ag_start(q, r, 3, 1, 0, 1, 0, -1)
            second_start(q, r, 1)
            second_start(q, r, 3)

    def first_end(q):
        for r in (0, 1):
            ag_wait(q, r, 2, 2, 0, 0)
            ag_wait(q, r, 3, 2, 0, 1)
            second_start(q, r, 2)

    def second_start(q, r, a):
        ag_start(q, r, 4 + 4 * a + 1, a, 0, None, 1, 1)
        ag_start(q, r, 4 + 4 * a, a, 0, None, 1, -1)

    def second_forward(q, a):
        for r in (0, 1):
            ag_wait(q, r, 4 + 4 * a + 1, a, 3, None)
            ag_start(q, r, 4 + 4 * a + 2, a, 3, 0, 1, 1)
            ag_wait(q, r, 4 + 4 * a, a, 1, None)
            ag_start(q, r, 4 + 4 * a + 3, a, 1, 1, 1, -1)

    def second_end(q, a):
        for r in (0, 1):
            ag_wait(q, r, 4 + 4 * a + 2, a, 2, 0)
            ag_wait(q, r, 4 + 4 * a + 3, a, 2, 1)

    first_start(0, 0)
    am_start(0)
    second_start(0, 0, 0)
    tok_pair = remote(tok_ref, xs.at[pl.ds(TOK, TOK)], pair_send.at[2], pair_recv.at[2], sibling)
    cot_pair = remote(cot_ref, cots.at[pl.ds(TOK, TOK)], pair_send.at[3], pair_recv.at[3], sibling)
    swap_copy(0, sib_rows).wait_recv()
    first_start(0, 1)
    second_start(0, 1, 0)
    tok_pair.start()
    cot_pair.start()
    am_finish(0)
    am_start(1)
    swap_copy(1, sib_rows).wait_recv()
    first_start(1, 0)
    first_start(1, 1)
    first_forward(0)
    second_start(1, 0, 0)
    second_start(1, 1, 0)

    tok_local.wait()
    tok_pair.wait_recv()

    @pl.loop(0, D // 128)
    def _(b):
        cols = pl.ds(pl.multiple_of(b * 128, 128), 128)
        xt[cols, :] = xs[:, cols].T

    second_forward(0, 0)
    am_finish(1)
    am_start(2)
    first_end(0)
    am_finish(2)
    am_start(3)
    second_forward(0, 1)
    second_forward(0, 3)
    am_finish(3)

    gate_max = jnp.max(am_mine[4, 0:4, :])
    up_max = jnp.max(am_mine[4, 4:8, :])
    amax_ref[0] = gate_max
    amax_ref[1] = up_max
    col = lax.broadcasted_iota(jnp.int32, (8, WIDTH), 1)
    is_gate = (col < 256) | ((col >= 512) & (col < 640)) | ((col >= 768) & (col < 832))
    scale = 448.0 / (jnp.where(is_gate, gate_max, up_max) + 1e-06)
    scales[0] = scale
    scales[1] = 1.0 / scale

    cot_local.wait()
    cot_pair.wait_recv()

    def chunks(q, chips, fresh=False):
        group = slice(GROUPS[q][0], sum(GROUPS[q]))
        rows = [pl.ds(pl.multiple_of(chip_at(*place) * CHIP_ROWS, CHIP_ROWS), CHIP_ROWS) for place in chips]
        for own in rows:
            wq[own, group] = (wraw[q][own].astype(F32) * scales[0, 0:1, group]).astype(BF16)

        @pl.loop(0, 2)
        def _(m):
            toks = pl.ds(pl.multiple_of(m * TOK, TOK), TOK)
            left = jnp.concatenate([xs[toks, own] for own in rows], axis=1)
            right = jnp.concatenate([wq[own, group] for own in rows], axis=0)
            part = jnp.dot(left, right, preferred_element_type=F32)
            h[toks, group] = part if fresh else h[toks, group] + part

    def chunks_near(q):
        chunks(q, ((0, 0), (1, 0), (3, 0), (0, 1), (0, 3)), fresh=True)

    def chunks_corner(q):
        chunks(q, ((1, 1), (1, 3), (3, 1), (3, 3)))

    def chunks_across(q, a):
        chunks(q, ((2, a), (a, 2)))

    low_tok = lax.broadcasted_iota(jnp.int32, (64, 128), 1) < 64

    def activation_grads(gate, up, cot):
        sig = jax.nn.sigmoid(gate)
        return cot * up * sig * (1.0 + gate * (1.0 - sig)), cot * gate * sig

    def hidden_grads(q):
        @pl.loop(0, 2 * TOK // 64)
        def _(m):
            toks = pl.ds(pl.multiple_of(m * 64, 64), 64)
            start, width = GROUPS[q]
            inv = scales[1, 0:1, start : start + width]
            hidden = h[toks, start : start + width] * inv
            main = 256 if q == 0 else 128
            cot = cots[toks, pl.ds(pl.multiple_of(c * 512 + 256 * q, 128), main)].astype(F32)
            dgate, dup = activation_grads(hidden[:, 0:main], hidden[:, main : 2 * main], cot)
            parts = [(0, main, dgate), (main, 2 * main, dup)]
            if q == 1:
                mixed = hidden[:, 256:384]
                block = cots[toks, MAIN : MAIN + 128].astype(F32)
                block = jnp.where(c == 0, block, pltpu.roll(block, 64, 1))
                mgate, mup = activation_grads(mixed, pltpu.roll(mixed, 64, 1), block)
                parts.append((256, 384, jnp.where(low_tok, mgate, pltpu.roll(mup, 64, 1))))
            for lo, hi, part in parts:
                g[toks, start + lo : start + hi] = part.astype(BF16)
                gs[toks, start + lo : start + hi] = (part * inv[:, lo:hi]).astype(BF16)

    def weight_grad(q, r, a, b):
        group = slice(GROUPS[q][0], sum(GROUPS[q]))
        return jnp.dot(xt[pl.ds(row_of(r, a, b), ROWS)], g[:, group], preferred_element_type=F32)

    def toward(r, axis, sign):
        return at(*place(r, *((sign % SIDE, 0) if axis == 0 else (0, sign % SIDE))))

    def s1_copy(q, r, a, part):
        return remote(
            s1buf[q].at[r, a, pl.ds(part * HALF, HALF)], s1in[q].at[r, a, part],
            s1_send.at[q, r, a, part], s1_recv.at[q, r, a, part], toward(r, 1, 1 - 2 * part),
        )

    def s2_copy(q, r, a, part):
        return remote(
            s2buf[q].at[r, a, part], s2in[q].at[r, a, part],
            s2_send.at[q, r, a, part], s2_recv.at[q, r, a, part], toward(r, 1, 1 - 2 * part),
        )

    def t1_copy(q, r, part):
        return remote(
            rbuf[q].at[r, 2, pl.ds(part * HALF, HALF)], t1in[q].at[r, part],
            t1_send.at[q, r, part], t1_recv.at[q, r, part], toward(r, 0, 1 - 2 * part),
        )

    def t2_copy(q, r, part):
        return remote(
            rbuf[q].at[r, 1 + 2 * part], t2in[q].at[r, part],
            t2_send.at[q, r, part], t2_recv.at[q, r, part], toward(r, 0, 1 - 2 * part),
        )

    def step1(q):
        for a in (2, 1, 3, 0):
            for r in (0, 1):
                s1buf[q][r, a] = weight_grad(q, r, a, 2).astype(BF16)
                s1_copy(q, r, a, 0).start()
                s1_copy(q, r, a, 1).start()

    chunks_near(0)
    first_forward(1)
    chunks_corner(0)
    second_end(0, 0)
    second_forward(0, 2)
    chunks_across(0, 0)
    second_forward(1, 0)
    chunks_near(1)
    for a in (1, 3):
        second_end(0, a)
        chunks_across(0, a)
    first_end(1)
    second_end(0, 2)
    chunks(0, ((2, 2),))
    hidden_grads(0)
    second_forward(1, 1)
    second_forward(1, 3)
    chunks_corner(1)
    second_end(1, 0)
    chunks_across(1, 0)
    second_forward(1, 2)
    step1(0)
    for a in (1, 3):
        second_end(1, a)
        chunks_across(1, a)
    second_end(1, 2)
    chunks(1, ((2, 2),))
    hidden_grads(1)
    step1(1)

    def p_copy(dz):
        return remote(p_send.at[dz], p_in.at[dz], p_ssem.at[dz], p_rsem.at[dz], sibling)

    def input_grads(k):
        odd = lax.rem(k, 2)
        dz = odd * (4 - lax.div(k + 1, 2)) + (1 - odd) * (4 + lax.div(k, 2))
        cols = pl.ds(pl.multiple_of(lax.rem(z + dz, DEPTH) * ZCOL, ZCOL), ZCOL)
        p_send[dz] = lax.dot_general(gs[TOK:, :], wq[cols], NT, preferred_element_type=F32).astype(BF16)
        p_copy(dz).start()
        p_own[dz] = lax.dot_general(gs[:TOK, :], wq[cols], NT, preferred_element_type=F32).astype(BF16)

    def added(out, total, part, extra):
        lo = slice(part * HALF, part * HALF + HALF)
        hi = slice((1 - part) * HALF, (1 - part) * HALF + HALF)
        out[lo] = (total[lo] + extra.astype(F32)).astype(BF16)
        out[hi] = total[hi].astype(BF16)

    def step2(a, halves=(0, 1), groups=(0, 1)):
        for q in groups:
            for r in halves:
                for part in (0, 1):
                    s1_copy(q, r, a, part).wait_recv()
                    grad = weight_grad(q, r, a, 1 + 2 * part)
                    added(s2buf[q].at[r, a, part], grad, part, s1in[q][r, a, part])
                    s2_copy(q, r, a, part).start()

    def reduced(q, r, a):
        s2_copy(q, r, a, 0).wait_recv()
        s2_copy(q, r, a, 1).wait_recv()
        return weight_grad(q, r, a, 0) + s2in[q][r, a, 0].astype(F32) + s2in[q][r, a, 1].astype(F32)

    def z1_copy(part):
        return remote(
            p_own.at[4, pl.ds(part * (TOK // 2), TOK // 2)], z1in.at[part],
            z1_send.at[part], z1_recv.at[part], at_z(1 if part == 0 else DEPTH - 1),
        )

    def z_copy(step, part):
        dz = (3 - step) if part == 0 else (5 + step)
        return remote(
            p_own.at[dz], zin.at[step, part],
            z_send.at[step, part], z_recv.at[step, part], at_z(1 if part == 0 else DEPTH - 1),
        )

    def pair_sum(dz):
        p_copy(dz).wait_recv()
        return p_own[dz].astype(F32) + p_in[dz].astype(F32)

    def z_first():
        p_own[4] = pair_sum(4).astype(BF16)
        z1_copy(0).start()
        z1_copy(1).start()

    def z_round(step):
        for part in (0, 1):
            dz = (3 - step) if part == 0 else (5 + step)
            total = pair_sum(dz)
            if step == 0:
                z1_copy(part).wait_recv()
                lo = slice(part * (TOK // 2), (part + 1) * (TOK // 2))
                hi = slice((1 - part) * (TOK // 2), (2 - part) * (TOK // 2))
                p_own[dz, lo] = (total[lo] + z1in[part].astype(F32)).astype(BF16)
                p_own[dz, hi] = total[hi].astype(BF16)
            else:
                z_copy(step - 1, part).wait_recv()
                p_own[dz] = (total + zin[step - 1, part].astype(F32)).astype(BF16)
            z_copy(step, part).start()

    def reduced_across(q):
        for r in (0, 1):
            rbuf[q][r, 2] = reduced(q, r, 2).astype(BF16)
            t1_copy(q, r, 0).start()
            t1_copy(q, r, 1).start()

    def later(q, r, part):
        total = reduced(q, r, 1 + 2 * part)
        t1_copy(q, r, part).wait_recv()
        added(rbuf[q].at[r, 1 + 2 * part], total, part, t1in[q][r, part])
        t2_copy(q, r, part).start()

    pl.loop(0, 1)(input_grads)
    step2(2)
    z_first()
    pl.loop(1, 3)(input_grads)
    step2(1)
    z_round(0)
    pl.loop(3, 5)(input_grads)
    reduced_across(0)
    reduced_across(1)
    step2(3)
    z_round(1)
    pl.loop(5, DEPTH)(input_grads)
    for q in (0, 1):
        swap_copy(q, own_rows).wait_send()
    tok_pair.wait_send()
    cot_pair.wait_send()
    for copy in started:
        copy.wait_send()
    for stage in range(len(stages)):
        for copy in am_copies(stage):
            copy.wait_send()
    step2(0, (1,))
    step2(0, (0,), (0,))
    for part in (0, 1):
        for q in (0, 1):
            later(q, 1, part)
    step2(0, (0,), (1,))
    z_round(2)
    for part in (0, 1):
        for q in (0, 1):
            later(q, 0, part)

    def finished(q, r):
        total = reduced(q, r, 0)
        t2_copy(q, r, 0).wait_recv()
        t2_copy(q, r, 1).wait_recv()
        return (total + t2in[q][r, 0].astype(F32) + t2in[q][r, 1].astype(F32)).astype(BF16)

    def last_copy(q):
        return remote(final[q].at[1], final_in[q], pair_send.at[4 + q], pair_recv.at[4 + q], sibling)

    for q in (0, 1):
        for r in (0, 1):
            for part in (0, 1):
                for a in range(SIDE):
                    s1_copy(q, r, a, part).wait_send()
                    if a or r:
                        s2_copy(q, r, a, part).wait_send()
                t1_copy(q, r, part).wait_send()
    for part in (0, 1):
        t2_copy(0, 1, part).wait_send()
        t2_copy(1, 1, part).wait_send()
        z1_copy(part).wait_send()
        z_copy(0, part).wait_send()
        z_copy(1, part).wait_send()
    for dz in range(DEPTH):
        p_copy(dz).wait_send()

    for q in (0, 1):
        final[q][1] = finished(q, 1)
        last_copy(q).start()
    total = pair_sum(0)
    z_copy(2, 0).wait_recv()
    z_copy(2, 1).wait_recv()
    ig_ref[...] = (total + zin[2, 0].astype(F32) + zin[2, 1].astype(F32)).astype(BF16)
    ig_out = pltpu.make_async_copy(ig_ref, ig_hbm, loc_sem.at[4])
    ig_out.start()
    for q in (0, 1):
        final[q][0] = finished(q, 0)

    def placed(ref, first):
        cols = pl.ds(first, 256)
        gg_ref[:, cols] = ref[0][:, 0:256]
        ug_ref[:, cols] = ref[0][:, 256:512]
        cols = pl.ds(pl.multiple_of(first + 256, 128), 128)
        gg_ref[:, cols] = ref[1][:, 0:128]
        ug_ref[:, cols] = ref[1][:, 128:256]
        return ref[1][:, 256:384].astype(F32)

    mine = placed([final[q].at[0] for q in (0, 1)], own_first)
    for q in (0, 1):
        last_copy(q).wait_recv()
    theirs = placed(final_in, sib_first)
    first = jnp.where(c == 0, mine, theirs)
    second = jnp.where(c == 0, theirs, mine)
    gg_ref[:, MAIN : MAIN + 128] = jnp.where(low, first, pltpu.roll(second, 64, 1)).astype(BF16)
    ug_ref[:, MAIN : MAIN + 128] = jnp.where(low, pltpu.roll(first, 64, 1), second).astype(BF16)

    outs = [
        ig_out,
        pltpu.make_async_copy(gg_ref, gg_hbm, loc_sem.at[5]),
        pltpu.make_async_copy(ug_ref, ug_hbm, loc_sem.at[6]),
    ]
    outs[1].start()
    outs[2].start()

    for q in (0, 1):
        last_copy(q).wait_send()
        for part in (0, 1):
            t2_copy(q, 0, part).wait_send()
            s2_copy(q, 0, 0, part).wait_send()
    for part in (0, 1):
        z_copy(2, part).wait_send()
    for copy in outs:
        copy.wait()


def hand_over(a_in, b_in, c_in, amax_in, a_out, b_out, c_out, amax_out):
    a_out[...] = a_in[...]
    b_out[...] = b_in[...]
    c_out[...] = c_in[...]
    amax_out[0] = amax_in[0]
    amax_out[1] = amax_in[1]


def on_device(tokens, cotangent, gate_weight, up_weight):
    vmem = pltpu.VMEM
    dma = pltpu.SemaphoreType.DMA

    def both(*shape):
        return tuple(vmem(shape + (width,), BF16) for _, width in GROUPS)

    scratch = [
        vmem((ROWS, WIDTH), BF16),
        vmem((ROWS, WIDTH), BF16),
        vmem((TOK, ZCOL), BF16),
        vmem((ROWS, WIDTH), BF16),
        vmem((ROWS, WIDTH), BF16),
        vmem((2 * TOK, D), BF16),
        vmem((D, 2 * TOK), BF16),
        vmem((2 * TOK, WIDTH), BF16),
        both(D),
        vmem((D, WIDTH), BF16),
        vmem((2 * TOK, WIDTH), F32),
        vmem((2 * TOK, WIDTH), BF16),
        vmem((2 * TOK, WIDTH), BF16),
        both(ROWS),
        vmem((2, 8, WIDTH), F32),
        vmem((5, 8, 128), F32),
        vmem((14, 8, 128), F32),
        both(2, SIDE, ROWS),
        both(2, SIDE, 2, HALF),
        both(2, SIDE, 2, ROWS),
        both(2, SIDE, 2, ROWS),
        both(2, SIDE, ROWS),
        both(2, 2, HALF),
        both(2, 2, ROWS),
        both(2, ROWS),
        both(ROWS),
        vmem((DEPTH, TOK, ZCOL), BF16),
        vmem((DEPTH, TOK, ZCOL), BF16),
        vmem((DEPTH, TOK, ZCOL), BF16),
        vmem((2, TOK // 2, ZCOL), BF16),
        vmem((3, 2, TOK, ZCOL), BF16),
        dma((7,)), dma((6,)), dma((6,)), dma((2, 2, 20)), dma((2, 2, 20)), dma((14,)), dma((14,)),
        dma((2, 2, SIDE, 2)), dma((2, 2, SIDE, 2)), dma((2, 2, SIDE, 2)), dma((2, 2, SIDE, 2)),
        dma((2, 2, 2)), dma((2, 2, 2)), dma((2, 2, 2)), dma((2, 2, 2)),
        dma((DEPTH,)), dma((DEPTH,)), dma((2,)), dma((2,)), dma((3, 2)), dma((3, 2)),
    ]
    anywhere = pl.BlockSpec(memory_space=pl.ANY)
    scalars = pl.BlockSpec(memory_space=pltpu.SMEM)
    whole = pl.BlockSpec(memory_space=pltpu.VMEM)
    outs = pl.pallas_call(
        kernel,
        out_shape=(
            jax.ShapeDtypeStruct((TOK, ZCOL), BF16),
            jax.ShapeDtypeStruct((ROWS, WIDTH), BF16),
            jax.ShapeDtypeStruct((ROWS, WIDTH), BF16),
            jax.ShapeDtypeStruct((2,), F32),
        ),
        in_specs=[anywhere] * 4,
        out_specs=(anywhere,) * 3 + (scalars,),
        scratch_shapes=scratch,
        compiler_params=pltpu.CompilerParams(
            collective_id=0, has_side_effects=True, vmem_limit_bytes=62 * 1024 * 1024
        ),
        cost_estimate=pl.CostEstimate(flops=3 * 2 * 512 * 4096 * 896, bytes_accessed=4 << 20, transcendentals=512 * 448),
        name="swiglu_backward",
    )(tokens, cotangent, gate_weight, up_weight)
    return pl.pallas_call(
        hand_over,
        out_shape=tuple(jax.ShapeDtypeStruct(o.shape, o.dtype) for o in outs),
        in_specs=[whole] * 3 + [scalars],
        out_specs=(whole,) * 3 + (scalars,),
        compiler_params=pltpu.CompilerParams(vmem_limit_bytes=62 * 1024 * 1024),
        name="hand_over",
    )(*outs)


def solution(mesh):
    in_specs = (P("fsdp", None), P("fsdp", "tp"), P("fsdp", "tp"), P("fsdp", "tp"))
    out_specs = (P("fsdp", "tp"), P("fsdp", "tp"), P("fsdp", "tp"), P())
    return jax.shard_map(
        on_device, mesh=mesh, in_specs=in_specs, out_specs=out_specs, check_vma=False
    )
```

```python
import jax
import jax.numpy as jnp
from jax import lax
from jax.experimental import pallas as pl
from jax.experimental.pallas import tpu as pltpu
from jax.sharding import PartitionSpec as P

MESH = pl.DeviceIdType.MESH
F32 = jnp.float32
BF16 = jnp.bfloat16
SIDE = 4
DEPTH = 8
ROWS = 128
HALF = ROWS // 2
CHIP_ROWS = 2 * ROWS
TOK = 256
D = 4096
WIDTH = 896
MAIN = 384
GROUPS = ((0, 512), (512, 384))
ZCOL = D // DEPTH
NT = (((1,), (1,)), ((), ()))


def kernel(
    tok_ref, cot_ref, wg_hbm, wu_hbm,
    ig_hbm, own0_hbm, own1_hbm, other0_hbm, other1_hbm, amax_hbm,
    wg_ref, wu_ref, ig_ref,
    xs, xt, cots, wraw, wq, h, g, gs, psib, scales, am_mine, am_in,
    s1buf, s1in, s2buf, s2in, rbuf, t1in, t2in, final, final_in,
    p_own, p_send, p_in, z1in, zin,
    loc_sem, pair_send, pair_recv, ag_send, ag_recv, am_send, am_recv,
    s1_send, s1_recv, s2_send, s2_recv, t1_send, t1_recv, t2_send, t2_recv,
    p_ssem, p_rsem, z1_send, z1_recv, z_send, z_recv,
):
    f = lax.axis_index("fsdp")
    z = lax.axis_index("tp")
    c = lax.rem(f, 2)
    chip = lax.div(f, 2)
    x = lax.div(chip, SIDE)
    y = lax.rem(chip, SIDE)

    def chip_at(dx, dy):
        return lax.rem(x + dx, SIDE) * SIDE + lax.rem(y + dy, SIDE)

    def at(dx, dy):
        return (chip_at(dx, dy) * 2 + c, z)

    def at_z(dz):
        return (f, lax.rem(z + dz, DEPTH))

    sibling = (chip * 2 + 1 - c, z)

    def place(r, a, b):
        return (a, b) if r == 0 else (b, a)

    def row_of(r, a, b):
        return pl.multiple_of(chip_at(*place(r, a, b)) * CHIP_ROWS + (c if r == 0 else 1 - c) * ROWS, ROWS)

    def remote(src, dst, ssem, rsem, device):
        return pltpu.make_async_remote_copy(
            src_ref=src, dst_ref=dst, send_sem=ssem, recv_sem=rsem, device_id=device, device_id_type=MESH
        )

    barrier = pltpu.get_barrier_semaphore()
    x_peers = [at(k, 0) for k in range(1, SIDE)]
    y_peers = [at(0, k) for k in range(1, SIDE)]
    z_peers = [at_z(k) for k in range(1, DEPTH)]
    peers = x_peers + y_peers + z_peers + [sibling]
    for peer in peers:
        pl.semaphore_signal(barrier, inc=1, device_id=peer, device_id_type=MESH)

    w_local = [
        pltpu.make_async_copy(wg_hbm, wg_ref, loc_sem.at[2]),
        pltpu.make_async_copy(wu_hbm, wu_ref, loc_sem.at[3]),
    ]
    for copy in w_local:
        copy.start()
    tok_local = pltpu.make_async_copy(tok_ref, xs.at[pl.ds(0, TOK)], loc_sem.at[0])
    tok_local.start()
    cot_local = pltpu.make_async_copy(cot_ref, cots.at[pl.ds(0, TOK)], loc_sem.at[1])
    cot_local.start()

    lane = lax.broadcasted_iota(jnp.int32, (ROWS, 128), 1)
    low = lane < 64

    def packed_mixed(core):
        g3 = wg_ref[:, MAIN : MAIN + 128].astype(F32)
        u3 = wu_ref[:, MAIN : MAIN + 128].astype(F32)
        first = jnp.where(low, g3, pltpu.roll(u3, 64, 1))
        second = jnp.where(low, pltpu.roll(g3, 64, 1), u3)
        return jnp.where(core == 0, first, second).astype(BF16)

    for copy in w_local:
        copy.wait()
    own_rows = pl.ds(row_of(0, 0, 0), ROWS)
    sib_rows = pl.ds(row_of(1, 0, 0), ROWS)

    def packed(out, rows, first, core):
        cols = pl.ds(first, 256)
        out[0][rows, 0:256] = wg_ref[:, cols]
        out[0][rows, 256:512] = wu_ref[:, cols]
        cols = pl.ds(pl.multiple_of(first + 256, 128), 128)
        out[1][rows, 0:128] = wg_ref[:, cols]
        out[1][rows, 128:256] = wu_ref[:, cols]
        out[1][rows, 256:384] = packed_mixed(core)

    own_first = pl.multiple_of(c * 512, 128)
    sib_first = pl.multiple_of((1 - c) * 512, 128)
    packed(psib, slice(0, ROWS), sib_first, 1 - c)
    packed(wraw, own_rows, own_first, c)

    am_rows = lax.broadcasted_iota(jnp.int32, (8, 128), 0)

    def largest(ref):
        return jnp.max(jnp.abs(ref[...].astype(F32)), keepdims=True)

    am_mine[0] = jnp.where(am_rows < 4, largest(wg_ref), largest(wu_ref))
    stages = [x_peers, y_peers, [sibling], z_peers]
    slots, used = [], 0
    for devices in stages:
        slots.append(range(used, used + len(devices)))
        used += len(devices)

    def am_copies(stage):
        return [
            remote(am_mine.at[stage], am_in.at[slot], am_send.at[slot], am_recv.at[slot], device)
            for device, slot in zip(stages[stage], slots[stage])
        ]

    def am_start(stage):
        for copy in am_copies(stage):
            copy.start()

    def am_finish(stage):
        best = am_mine[stage]
        for copy in am_copies(stage):
            copy.wait_recv()
        for slot in slots[stage]:
            best = jnp.maximum(best, am_in[slot])
        am_mine[stage + 1] = best

    pl.semaphore_wait(barrier, len(peers))

    def swap_copy(q, rows):
        return remote(psib[q], wraw[q].at[rows], pair_send.at[q], pair_recv.at[q], sibling)

    for q in (0, 1):
        swap_copy(q, own_rows).start()

    def ag_copy(q, r, slot, a, b, part, axis, sign):
        rows = row_of(r, a, b)
        if part is None:
            rows, count = rows, ROWS
        else:
            rows, count = rows + part * HALF, HALF
        ref = wraw[q].at[pl.ds(pl.multiple_of(rows, HALF), count)]
        step = (sign % SIDE, 0) if axis == 0 else (0, sign % SIDE)
        return remote(ref, ref, ag_send.at[q, r, slot], ag_recv.at[q, r, slot], at(*place(r, *step)))

    started = []

    def ag_start(*args):
        copy = ag_copy(*args)
        copy.start()
        started.append(copy)

    def ag_wait(q, r, slot, a, b, part):
        ag_copy(q, r, slot, a, b, part, 0, 1).wait_recv()

    def first_start(q, r):
        ag_start(q, r, 1, 0, 0, None, 0, 1)
        ag_start(q, r, 0, 0, 0, None, 0, -1)

    def first_forward(q):
        for r in (0, 1):
            ag_wait(q, r, 1, 3, 0, None)
            ag_start(q, r, 2, 3, 0, 0, 0, 1)
            ag_wait(q, r, 0, 1, 0, None)
            ag_start(q, r, 3, 1, 0, 1, 0, -1)
            second_start(q, r, 1)
            second_start(q, r, 3)

    def first_end(q):
        for r in (0, 1):
            ag_wait(q, r, 2, 2, 0, 0)
            ag_wait(q, r, 3, 2, 0, 1)
            second_start(q, r, 2)

    def second_start(q, r, a):
        ag_start(q, r, 4 + 4 * a + 1, a, 0, None, 1, 1)
        ag_start(q, r, 4 + 4 * a, a, 0, None, 1, -1)

    def second_forward(q, a):
        for r in (0, 1):
            ag_wait(q, r, 4 + 4 * a + 1, a, 3, None)
            ag_start(q, r, 4 + 4 * a + 2, a, 3, 0, 1, 1)
            ag_wait(q, r, 4 + 4 * a, a, 1, None)
            ag_start(q, r, 4 + 4 * a + 3, a, 1, 1, 1, -1)

    def second_end(q, a):
        for r in (0, 1):
            ag_wait(q, r, 4 + 4 * a + 2, a, 2, 0)
            ag_wait(q, r, 4 + 4 * a + 3, a, 2, 1)

    first_start(0, 0)
    am_start(0)
    second_start(0, 0, 0)
    tok_pair = remote(tok_ref, xs.at[pl.ds(TOK, TOK)], pair_send.at[2], pair_recv.at[2], sibling)
    cot_pair = remote(cot_ref, cots.at[pl.ds(TOK, TOK)], pair_send.at[3], pair_recv.at[3], sibling)
    swap_copy(0, sib_rows).wait_recv()
    first_start(0, 1)
    second_start(0, 1, 0)
    tok_pair.start()
    cot_pair.start()
    am_finish(0)
    am_start(1)
    swap_copy(1, sib_rows).wait_recv()
    first_start(1, 0)
    first_start(1, 1)

    def transpose(first):
        @pl.loop(0, D // 256)
        def _(b):
            cols = pl.ds(pl.multiple_of(b * 256, 256), 256)
            xt[cols, first : first + TOK] = xs[first : first + TOK, cols].T

    tok_local.wait()
    transpose(0)
    first_forward(0)
    second_start(1, 0, 0)
    second_start(1, 1, 0)
    second_forward(0, 0)
    am_finish(1)
    am_start(2)
    first_end(0)
    am_finish(2)
    am_start(3)
    tok_pair.wait_recv()
    transpose(TOK)
    second_forward(0, 1)
    second_forward(0, 3)
    am_finish(3)

    gate_max = jnp.max(am_mine[4, 0:4, :])
    up_max = jnp.max(am_mine[4, 4:8, :])
    amax_out = pltpu.make_async_copy(am_mine.at[4], amax_hbm, loc_sem.at[7])
    amax_out.start()
    col = lax.broadcasted_iota(jnp.int32, (8, WIDTH), 1)
    is_gate = (col < 256) | ((col >= 512) & (col < 640)) | ((col >= 768) & (col < 832))
    scale = 448.0 / (jnp.where(is_gate, gate_max, up_max) + 1e-06)
    scales[0] = scale
    scales[1] = 1.0 / scale

    cot_local.wait()
    cot_pair.wait_recv()

    def chunks(q, chips, fresh=False):
        group = slice(GROUPS[q][0], sum(GROUPS[q]))
        rows = [pl.ds(pl.multiple_of(chip_at(*place) * CHIP_ROWS, CHIP_ROWS), CHIP_ROWS) for place in chips]
        for own in rows:
            wq[own, group] = (wraw[q][own].astype(F32) * scales[0, 0:1, group]).astype(BF16)

        @pl.loop(0, 2)
        def _(m):
            toks = pl.ds(pl.multiple_of(m * TOK, TOK), TOK)
            left = jnp.concatenate([xs[toks, own] for own in rows], axis=1)
            right = jnp.concatenate([wq[own, group] for own in rows], axis=0)
            part = jnp.dot(left, right, preferred_element_type=F32)
            h[toks, group] = part if fresh else h[toks, group] + part

    def chunks_near(q):
        chunks(q, ((0, 0), (1, 0), (3, 0), (0, 1), (0, 3)), fresh=True)

    def chunks_corner(q):
        chunks(q, ((1, 1), (1, 3), (3, 1), (3, 3)))

    def chunks_across(q, a):
        chunks(q, ((2, a), (a, 2)))

    low_tok = lax.broadcasted_iota(jnp.int32, (64, 128), 1) < 64

    def activation_grads(gate, up, cot):
        sig = jax.nn.sigmoid(gate)
        return cot * up * sig * (1.0 + gate * (1.0 - sig)), cot * gate * sig

    def hidden_grads(q):
        @pl.loop(0, 2 * TOK // 64)
        def _(m):
            toks = pl.ds(pl.multiple_of(m * 64, 64), 64)
            start, width = GROUPS[q]
            inv = scales[1, 0:1, start : start + width]
            hidden = h[toks, start : start + width] * inv
            main = 256 if q == 0 else 128
            cot = cots[toks, pl.ds(pl.multiple_of(c * 512 + 256 * q, 128), main)].astype(F32)
            dgate, dup = activation_grads(hidden[:, 0:main], hidden[:, main : 2 * main], cot)
            parts = [(0, main, dgate), (main, 2 * main, dup)]
            if q == 1:
                mixed = hidden[:, 256:384]
                block = cots[toks, MAIN : MAIN + 128].astype(F32)
                block = jnp.where(c == 0, block, pltpu.roll(block, 64, 1))
                mgate, mup = activation_grads(mixed, pltpu.roll(mixed, 64, 1), block)
                parts.append((256, 384, jnp.where(low_tok, mgate, pltpu.roll(mup, 64, 1))))
            for lo, hi, part in parts:
                g[toks, start + lo : start + hi] = part.astype(BF16)
                gs[toks, start + lo : start + hi] = (part * inv[:, lo:hi]).astype(BF16)

    def weight_grad(q, r, a, b):
        group = slice(GROUPS[q][0], sum(GROUPS[q]))
        return jnp.dot(xt[pl.ds(row_of(r, a, b), ROWS)], g[:, group], preferred_element_type=F32)

    def toward(r, axis, sign):
        return at(*place(r, *((sign % SIDE, 0) if axis == 0 else (0, sign % SIDE))))

    def s1_copy(q, r, a, part):
        return remote(
            s1buf[q].at[r, a, pl.ds(part * HALF, HALF)], s1in[q].at[r, a, part],
            s1_send.at[q, r, a, part], s1_recv.at[q, r, a, part], toward(r, 1, 1 - 2 * part),
        )

    def s2_copy(q, r, a, part):
        return remote(
            s2buf[q].at[r, a, part], s2in[q].at[r, a, part],
            s2_send.at[q, r, a, part], s2_recv.at[q, r, a, part], toward(r, 1, 1 - 2 * part),
        )

    def t1_copy(q, r, part):
        return remote(
            rbuf[q].at[r, 2, pl.ds(part * HALF, HALF)], t1in[q].at[r, part],
            t1_send.at[q, r, part], t1_recv.at[q, r, part], toward(r, 0, 1 - 2 * part),
        )

    def t2_copy(q, r, part):
        return remote(
            rbuf[q].at[r, 1 + 2 * part], t2in[q].at[r, part],
            t2_send.at[q, r, part], t2_recv.at[q, r, part], toward(r, 0, 1 - 2 * part),
        )

    def step1(q):
        for a in (2, 1, 3, 0):
            for r in (0, 1):
                s1buf[q][r, a] = weight_grad(q, r, a, 2).astype(BF16)
                s1_copy(q, r, a, 0).start()
                s1_copy(q, r, a, 1).start()

    chunks_near(0)
    first_forward(1)
    chunks_corner(0)
    second_end(0, 0)
    second_forward(0, 2)
    chunks_across(0, 0)
    second_forward(1, 0)
    chunks_near(1)
    for a in (1, 3):
        second_end(0, a)
        chunks_across(0, a)
    first_end(1)
    second_end(0, 2)
    chunks(0, ((2, 2),))
    hidden_grads(0)
    second_forward(1, 1)
    second_forward(1, 3)
    chunks_corner(1)
    second_end(1, 0)
    chunks_across(1, 0)
    second_forward(1, 2)
    step1(0)
    for a in (1, 3):
        second_end(1, a)
        chunks_across(1, a)
    second_end(1, 2)
    chunks(1, ((2, 2),))
    hidden_grads(1)
    step1(1)

    def p_copy(dz):
        return remote(p_send.at[dz], p_in.at[dz], p_ssem.at[dz], p_rsem.at[dz], sibling)

    def input_grads(k):
        odd = lax.rem(k, 2)
        dz = odd * (4 - lax.div(k + 1, 2)) + (1 - odd) * (4 + lax.div(k, 2))
        cols = pl.ds(pl.multiple_of(lax.rem(z + dz, DEPTH) * ZCOL, ZCOL), ZCOL)
        p_send[dz] = lax.dot_general(gs[TOK:, :], wq[cols], NT, preferred_element_type=F32).astype(BF16)
        p_copy(dz).start()
        p_own[dz] = lax.dot_general(gs[:TOK, :], wq[cols], NT, preferred_element_type=F32).astype(BF16)

    def added(out, total, part, extra):
        lo = slice(part * HALF, part * HALF + HALF)
        hi = slice((1 - part) * HALF, (1 - part) * HALF + HALF)
        out[lo] = (total[lo] + extra.astype(F32)).astype(BF16)
        out[hi] = total[hi].astype(BF16)

    def step2(a, halves=(0, 1), groups=(0, 1)):
        for q in groups:
            for r in halves:
                for part in (0, 1):
                    s1_copy(q, r, a, part).wait_recv()
                    grad = weight_grad(q, r, a, 1 + 2 * part)
                    added(s2buf[q].at[r, a, part], grad, part, s1in[q][r, a, part])
                    s2_copy(q, r, a, part).start()

    def reduced(q, r, a):
        s2_copy(q, r, a, 0).wait_recv()
        s2_copy(q, r, a, 1).wait_recv()
        return weight_grad(q, r, a, 0) + s2in[q][r, a, 0].astype(F32) + s2in[q][r, a, 1].astype(F32)

    def z1_copy(part):
        return remote(
            p_own.at[4, pl.ds(part * (TOK // 2), TOK // 2)], z1in.at[part],
            z1_send.at[part], z1_recv.at[part], at_z(1 if part == 0 else DEPTH - 1),
        )

    def z_copy(step, part):
        dz = (3 - step) if part == 0 else (5 + step)
        return remote(
            p_own.at[dz], zin.at[step, part],
            z_send.at[step, part], z_recv.at[step, part], at_z(1 if part == 0 else DEPTH - 1),
        )

    def pair_sum(dz):
        p_copy(dz).wait_recv()
        return p_own[dz].astype(F32) + p_in[dz].astype(F32)

    def z_first():
        p_own[4] = pair_sum(4).astype(BF16)
        z1_copy(0).start()
        z1_copy(1).start()

    def z_round(step):
        for part in (0, 1):
            dz = (3 - step) if part == 0 else (5 + step)
            total = pair_sum(dz)
            if step == 0:
                z1_copy(part).wait_recv()
                lo = slice(part * (TOK // 2), (part + 1) * (TOK // 2))
                hi = slice((1 - part) * (TOK // 2), (2 - part) * (TOK // 2))
                p_own[dz, lo] = (total[lo] + z1in[part].astype(F32)).astype(BF16)
                p_own[dz, hi] = total[hi].astype(BF16)
            else:
                z_copy(step - 1, part).wait_recv()
                p_own[dz] = (total + zin[step - 1, part].astype(F32)).astype(BF16)
            z_copy(step, part).start()

    def reduced_across(q):
        for r in (0, 1):
            rbuf[q][r, 2] = reduced(q, r, 2).astype(BF16)
            t1_copy(q, r, 0).start()
            t1_copy(q, r, 1).start()

    def later(q, r, part):
        total = reduced(q, r, 1 + 2 * part)
        t1_copy(q, r, part).wait_recv()
        added(rbuf[q].at[r, 1 + 2 * part], total, part, t1in[q][r, part])
        t2_copy(q, r, part).start()

    pl.loop(0, 1)(input_grads)
    step2(2)
    z_first()
    pl.loop(1, 3)(input_grads)
    step2(1)
    z_round(0)
    pl.loop(3, 5)(input_grads)
    reduced_across(0)
    reduced_across(1)
    step2(3)
    z_round(1)
    pl.loop(5, DEPTH)(input_grads)
    for q in (0, 1):
        swap_copy(q, own_rows).wait_send()
    tok_pair.wait_send()
    cot_pair.wait_send()
    for copy in started:
        copy.wait_send()
    for stage in range(len(stages)):
        for copy in am_copies(stage):
            copy.wait_send()
    step2(0, (1,))
    step2(0, (0,), (0,))
    for part in (0, 1):
        for q in (0, 1):
            later(q, 1, part)
    step2(0, (0,), (1,))
    z_round(2)
    for part in (0, 1):
        for q in (0, 1):
            later(q, 0, part)

    def finished(q, r):
        total = reduced(q, r, 0)
        t2_copy(q, r, 0).wait_recv()
        t2_copy(q, r, 1).wait_recv()
        return (total + t2in[q][r, 0].astype(F32) + t2in[q][r, 1].astype(F32)).astype(BF16)

    def last_copy(q):
        return remote(final[q].at[1], final_in[q], pair_send.at[4 + q], pair_recv.at[4 + q], sibling)

    for q in (0, 1):
        for r in (0, 1):
            for part in (0, 1):
                for a in range(SIDE):
                    s1_copy(q, r, a, part).wait_send()
                    if a or r:
                        s2_copy(q, r, a, part).wait_send()
                t1_copy(q, r, part).wait_send()
    for part in (0, 1):
        t2_copy(0, 1, part).wait_send()
        t2_copy(1, 1, part).wait_send()
        z1_copy(part).wait_send()
        z_copy(0, part).wait_send()
        z_copy(1, part).wait_send()
    for dz in range(DEPTH):
        p_copy(dz).wait_send()

    for q in (0, 1):
        final[q][1] = finished(q, 1)
        last_copy(q).start()
    total = pair_sum(0)
    z_copy(2, 0).wait_recv()
    z_copy(2, 1).wait_recv()
    ig_ref[...] = (total + zin[2, 0].astype(F32) + zin[2, 1].astype(F32)).astype(BF16)
    ig_out = pltpu.make_async_copy(ig_ref, ig_hbm, loc_sem.at[4])
    ig_out.start()
    outs = [amax_out, ig_out]
    for q, (own_hbm, other_hbm) in enumerate(((own0_hbm, other0_hbm), (own1_hbm, other1_hbm))):
        last_copy(q).wait_recv()
        outs.append(pltpu.make_async_copy(final_in[q], other_hbm, loc_sem.at[5 + q]))
        outs[-1].start()
        final[q][0] = finished(q, 0)
        outs.append(pltpu.make_async_copy(final[q].at[0], own_hbm, loc_sem.at[8 + q]))
        outs[-1].start()

    for q in (0, 1):
        last_copy(q).wait_send()
        for part in (0, 1):
            t2_copy(q, 0, part).wait_send()
            s2_copy(q, 0, 0, part).wait_send()
    for part in (0, 1):
        z_copy(2, part).wait_send()
    for copy in outs:
        copy.wait()


def hand_over(ig_in, own0, own1, other0, other1, amax_in, ig_out, gg_out, ug_out, amax_out):
    c = lax.rem(lax.axis_index("fsdp"), 2)
    low = lax.broadcasted_iota(jnp.int32, (ROWS, 128), 1) < 64
    ig_out[...] = ig_in[...]

    def placed(group0, group1, first):
        cols = pl.ds(first, 256)
        gg_out[:, cols] = group0[:, 0:256]
        ug_out[:, cols] = group0[:, 256:512]
        cols = pl.ds(pl.multiple_of(first + 256, 128), 128)
        gg_out[:, cols] = group1[:, 0:128]
        ug_out[:, cols] = group1[:, 128:256]
        return group1[:, 256:384].astype(F32)

    mine = placed(own0, own1, pl.multiple_of(c * 512, 128))
    theirs = placed(other0, other1, pl.multiple_of((1 - c) * 512, 128))
    first = jnp.where(c == 0, mine, theirs)
    second = jnp.where(c == 0, theirs, mine)
    gg_out[:, MAIN : MAIN + 128] = jnp.where(low, first, pltpu.roll(second, 64, 1)).astype(BF16)
    ug_out[:, MAIN : MAIN + 128] = jnp.where(low, pltpu.roll(first, 64, 1), second).astype(BF16)
    amax_out[0] = jnp.max(amax_in[0:4, :])
    amax_out[1] = jnp.max(amax_in[4:8, :])


def on_device(tokens, cotangent, gate_weight, up_weight):
    vmem = pltpu.VMEM
    dma = pltpu.SemaphoreType.DMA

    def both(*shape):
        return tuple(vmem(shape + (width,), BF16) for _, width in GROUPS)

    scratch = [
        vmem((ROWS, WIDTH), BF16),
        vmem((ROWS, WIDTH), BF16),
        vmem((TOK, ZCOL), BF16),
        vmem((2 * TOK, D), BF16),
        vmem((D, 2 * TOK), BF16),
        vmem((2 * TOK, WIDTH), BF16),
        both(D),
        vmem((D, WIDTH), BF16),
        vmem((2 * TOK, WIDTH), F32),
        vmem((2 * TOK, WIDTH), BF16),
        vmem((2 * TOK, WIDTH), BF16),
        both(ROWS),
        vmem((2, 8, WIDTH), F32),
        vmem((5, 8, 128), F32),
        vmem((14, 8, 128), F32),
        both(2, SIDE, ROWS),
        both(2, SIDE, 2, HALF),
        both(2, SIDE, 2, ROWS),
        both(2, SIDE, 2, ROWS),
        both(2, SIDE, ROWS),
        both(2, 2, HALF),
        both(2, 2, ROWS),
        both(2, ROWS),
        both(ROWS),
        vmem((DEPTH, TOK, ZCOL), BF16),
        vmem((DEPTH, TOK, ZCOL), BF16),
        vmem((DEPTH, TOK, ZCOL), BF16),
        vmem((2, TOK // 2, ZCOL), BF16),
        vmem((3, 2, TOK, ZCOL), BF16),
        dma((10,)), dma((6,)), dma((6,)), dma((2, 2, 20)), dma((2, 2, 20)), dma((14,)), dma((14,)),
        dma((2, 2, SIDE, 2)), dma((2, 2, SIDE, 2)), dma((2, 2, SIDE, 2)), dma((2, 2, SIDE, 2)),
        dma((2, 2, 2)), dma((2, 2, 2)), dma((2, 2, 2)), dma((2, 2, 2)),
        dma((DEPTH,)), dma((DEPTH,)), dma((2,)), dma((2,)), dma((3, 2)), dma((3, 2)),
    ]
    anywhere = pl.BlockSpec(memory_space=pl.ANY)
    scalars = pl.BlockSpec(memory_space=pltpu.SMEM)
    whole = pl.BlockSpec(memory_space=pltpu.VMEM)
    outs = pl.pallas_call(
        kernel,
        out_shape=(
            jax.ShapeDtypeStruct((TOK, ZCOL), BF16),
            jax.ShapeDtypeStruct((ROWS, GROUPS[0][1]), BF16),
            jax.ShapeDtypeStruct((ROWS, GROUPS[1][1]), BF16),
            jax.ShapeDtypeStruct((ROWS, GROUPS[0][1]), BF16),
            jax.ShapeDtypeStruct((ROWS, GROUPS[1][1]), BF16),
            jax.ShapeDtypeStruct((8, 128), F32),
        ),
        in_specs=[anywhere] * 4,
        out_specs=(anywhere,) * 6,
        scratch_shapes=scratch,
        compiler_params=pltpu.CompilerParams(
            collective_id=0, has_side_effects=True, vmem_limit_bytes=62 * 1024 * 1024
        ),
        cost_estimate=pl.CostEstimate(flops=3 * 2 * 512 * 4096 * 896, bytes_accessed=4 << 20, transcendentals=512 * 448),
        name="swiglu_backward",
    )(tokens, cotangent, gate_weight, up_weight)
    return pl.pallas_call(
        hand_over,
        out_shape=(
            jax.ShapeDtypeStruct((TOK, ZCOL), BF16),
            jax.ShapeDtypeStruct((ROWS, WIDTH), BF16),
            jax.ShapeDtypeStruct((ROWS, WIDTH), BF16),
            jax.ShapeDtypeStruct((2,), F32),
        ),
        in_specs=[whole] * 6,
        out_specs=(whole,) * 3 + (scalars,),
        compiler_params=pltpu.CompilerParams(vmem_limit_bytes=62 * 1024 * 1024),
        name="hand_over",
    )(*outs)


def solution(mesh):
    in_specs = (P("fsdp", None), P("fsdp", "tp"), P("fsdp", "tp"), P("fsdp", "tp"))
    out_specs = (P("fsdp", "tp"), P("fsdp", "tp"), P("fsdp", "tp"), P())
    return jax.shard_map(
        on_device, mesh=mesh, in_specs=in_specs, out_specs=out_specs, check_vma=False
    )
```

```python
import jax
import jax.numpy as jnp
from jax import lax
from jax.experimental import pallas as pl
from jax.experimental.pallas import tpu as pltpu
from jax.sharding import PartitionSpec as P

MESH = pl.DeviceIdType.MESH
F32 = jnp.float32
BF16 = jnp.bfloat16
SIDE = 4
DEPTH = 8
ROWS = 128
HALF = ROWS // 2
CHIP_ROWS = 2 * ROWS
TOK = 256
D = 4096
WIDTH = 896
MAIN = 384
GROUPS = ((0, 512), (512, 384))
ZCOL = D // DEPTH
NT = (((1,), (1,)), ((), ()))


def kernel(
    tok_ref, cot_ref, wg_hbm, wu_hbm,
    ig_hbm, own0_hbm, own1_hbm, other0_hbm, other1_hbm, amax_hbm,
    wg_ref, wu_ref, ig_ref,
    xs, xt, cots, wraw, wq, h, g, gs, psib, scales, am_mine, am_in,
    s1buf, s1in, s2buf, s2in, rbuf, t1in, t2in, final, final_in,
    p_own, p_send, p_in, z1in, zin,
    loc_sem, pair_send, pair_recv, ag_send, ag_recv, am_send, am_recv,
    s1_send, s1_recv, s2_send, s2_recv, t1_send, t1_recv, t2_send, t2_recv,
    p_ssem, p_rsem, z1_send, z1_recv, z_send, z_recv,
):
    f = lax.axis_index("fsdp")
    z = lax.axis_index("tp")
    c = lax.rem(f, 2)
    chip = lax.div(f, 2)
    x = lax.div(chip, SIDE)
    y = lax.rem(chip, SIDE)

    def chip_at(dx, dy):
        return lax.rem(x + dx, SIDE) * SIDE + lax.rem(y + dy, SIDE)

    def at(dx, dy):
        return (chip_at(dx, dy) * 2 + c, z)

    def at_z(dz):
        return (f, lax.rem(z + dz, DEPTH))

    sibling = (chip * 2 + 1 - c, z)

    def place(r, a, b):
        return (a, b) if r == 0 else (b, a)

    def row_of(r, a, b):
        return pl.multiple_of(chip_at(*place(r, a, b)) * CHIP_ROWS + (c if r == 0 else 1 - c) * ROWS, ROWS)

    def remote(src, dst, ssem, rsem, device):
        return pltpu.make_async_remote_copy(
            src_ref=src, dst_ref=dst, send_sem=ssem, recv_sem=rsem, device_id=device, device_id_type=MESH
        )

    barrier = pltpu.get_barrier_semaphore()
    x_peers = [at(k, 0) for k in range(1, SIDE)]
    y_peers = [at(0, k) for k in range(1, SIDE)]
    z_peers = [at_z(k) for k in range(1, DEPTH)]
    peers = x_peers + y_peers + z_peers + [sibling]
    for peer in peers:
        pl.semaphore_signal(barrier, inc=1, device_id=peer, device_id_type=MESH)

    w_local = [
        pltpu.make_async_copy(wg_hbm, wg_ref, loc_sem.at[2]),
        pltpu.make_async_copy(wu_hbm, wu_ref, loc_sem.at[3]),
    ]
    for copy in w_local:
        copy.start()
    tok_local = pltpu.make_async_copy(tok_ref, xs.at[pl.ds(0, TOK)], loc_sem.at[0])
    tok_local.start()
    cot_local = pltpu.make_async_copy(cot_ref, cots.at[pl.ds(0, TOK)], loc_sem.at[1])
    cot_local.start()

    lane = lax.broadcasted_iota(jnp.int32, (ROWS, 128), 1)
    low = lane < 64

    def packed_mixed(core):
        g3 = wg_ref[:, MAIN : MAIN + 128].astype(F32)
        u3 = wu_ref[:, MAIN : MAIN + 128].astype(F32)
        first = jnp.where(low, g3, pltpu.roll(u3, 64, 1))
        second = jnp.where(low, pltpu.roll(g3, 64, 1), u3)
        return jnp.where(core == 0, first, second).astype(BF16)

    for copy in w_local:
        copy.wait()
    own_rows = pl.ds(row_of(0, 0, 0), ROWS)
    sib_rows = pl.ds(row_of(1, 0, 0), ROWS)

    def packed(out, rows, first, core):
        cols = pl.ds(first, 256)
        out[0][rows, 0:256] = wg_ref[:, cols]
        out[0][rows, 256:512] = wu_ref[:, cols]
        cols = pl.ds(pl.multiple_of(first + 256, 128), 128)
        out[1][rows, 0:128] = wg_ref[:, cols]
        out[1][rows, 128:256] = wu_ref[:, cols]
        out[1][rows, 256:384] = packed_mixed(core)

    own_first = pl.multiple_of(c * 512, 128)
    sib_first = pl.multiple_of((1 - c) * 512, 128)
    packed(psib, slice(0, ROWS), sib_first, 1 - c)
    packed(wraw, own_rows, own_first, c)

    am_rows = lax.broadcasted_iota(jnp.int32, (8, 128), 0)

    def largest(ref):
        return jnp.max(jnp.abs(ref[...].astype(F32)), keepdims=True)

    am_mine[0] = jnp.where(am_rows < 4, largest(wg_ref), largest(wu_ref))
    stages = [x_peers, y_peers, [sibling], z_peers]
    slots, used = [], 0
    for devices in stages:
        slots.append(range(used, used + len(devices)))
        used += len(devices)

    def am_copies(stage):
        return [
            remote(am_mine.at[stage], am_in.at[slot], am_send.at[slot], am_recv.at[slot], device)
            for device, slot in zip(stages[stage], slots[stage])
        ]

    def am_start(stage):
        for copy in am_copies(stage):
            copy.start()

    def am_finish(stage):
        best = am_mine[stage]
        for copy in am_copies(stage):
            copy.wait_recv()
        for slot in slots[stage]:
            best = jnp.maximum(best, am_in[slot])
        am_mine[stage + 1] = best

    pl.semaphore_wait(barrier, len(peers))

    def swap_copy(q, rows):
        return remote(psib[q], wraw[q].at[rows], pair_send.at[q], pair_recv.at[q], sibling)

    for q in (0, 1):
        swap_copy(q, own_rows).start()

    def ag_copy(q, r, slot, a, b, part, axis, sign):
        rows = row_of(r, a, b)
        if part is None:
            rows, count = rows, ROWS
        else:
            rows, count = rows + part * HALF, HALF
        ref = wraw[q].at[pl.ds(pl.multiple_of(rows, HALF), count)]
        step = (sign % SIDE, 0) if axis == 0 else (0, sign % SIDE)
        return remote(ref, ref, ag_send.at[q, r, slot], ag_recv.at[q, r, slot], at(*place(r, *step)))

    started = []

    def ag_start(*args):
        copy = ag_copy(*args)
        copy.start()
        started.append(copy)

    def ag_wait(q, r, slot, a, b, part):
        ag_copy(q, r, slot, a, b, part, 0, 1).wait_recv()

    def first_start(q, r):
        ag_start(q, r, 1, 0, 0, None, 0, 1)
        ag_start(q, r, 0, 0, 0, None, 0, -1)

    def first_forward(q):
        for r in (0, 1):
            ag_wait(q, r, 1, 3, 0, None)
            ag_start(q, r, 2, 3, 0, 0, 0, 1)
            ag_wait(q, r, 0, 1, 0, None)
            ag_start(q, r, 3, 1, 0, 1, 0, -1)
            second_start(q, r, 1)
            second_start(q, r, 3)

    def first_end(q):
        for r in (0, 1):
            ag_wait(q, r, 2, 2, 0, 0)
            ag_wait(q, r, 3, 2, 0, 1)
            second_start(q, r, 2)

    def second_start(q, r, a):
        ag_start(q, r, 4 + 4 * a + 1, a, 0, None, 1, 1)
        ag_start(q, r, 4 + 4 * a, a, 0, None, 1, -1)

    def second_forward(q, a):
        for r in (0, 1):
            ag_wait(q, r, 4 + 4 * a + 1, a, 3, None)
            ag_start(q, r, 4 + 4 * a + 2, a, 3, 0, 1, 1)
            ag_wait(q, r, 4 + 4 * a, a, 1, None)
            ag_start(q, r, 4 + 4 * a + 3, a, 1, 1, 1, -1)

    def second_end(q, a):
        for r in (0, 1):
            ag_wait(q, r, 4 + 4 * a + 2, a, 2, 0)
            ag_wait(q, r, 4 + 4 * a + 3, a, 2, 1)

    first_start(0, 0)
    am_start(0)
    second_start(0, 0, 0)
    tok_pair = remote(tok_ref, xs.at[pl.ds(TOK, TOK)], pair_send.at[2], pair_recv.at[2], sibling)
    cot_pair = remote(cot_ref, cots.at[pl.ds(TOK, TOK)], pair_send.at[3], pair_recv.at[3], sibling)
    swap_copy(0, sib_rows).wait_recv()
    first_start(0, 1)
    second_start(0, 1, 0)
    tok_pair.start()
    cot_pair.start()
    am_finish(0)
    am_start(1)
    swap_copy(1, sib_rows).wait_recv()
    first_start(1, 0)
    first_start(1, 1)

    def transpose(first):
        @pl.loop(0, D // 256)
        def _(b):
            cols = pl.ds(pl.multiple_of(b * 256, 256), 256)
            xt[cols, first : first + TOK] = xs[first : first + TOK, cols].T

    tok_local.wait()
    transpose(0)
    first_forward(0)
    second_start(1, 0, 0)
    second_start(1, 1, 0)
    second_forward(0, 0)
    am_finish(1)
    am_start(2)
    first_end(0)
    am_finish(2)
    am_start(3)
    tok_pair.wait_recv()
    transpose(TOK)
    second_forward(0, 1)
    second_forward(0, 3)
    am_finish(3)

    gate_max = jnp.max(am_mine[4, 0:4, :])
    up_max = jnp.max(am_mine[4, 4:8, :])
    amax_out = pltpu.make_async_copy(am_mine.at[4], amax_hbm, loc_sem.at[7])
    amax_out.start()
    col = lax.broadcasted_iota(jnp.int32, (8, WIDTH), 1)
    is_gate = (col < 256) | ((col >= 512) & (col < 640)) | ((col >= 768) & (col < 832))
    scale = 448.0 / (jnp.where(is_gate, gate_max, up_max) + 1e-06)
    scales[0] = scale
    scales[1] = 1.0 / scale

    cot_local.wait()
    cot_pair.wait_recv()

    def chunks(q, chips, fresh=False):
        group = slice(GROUPS[q][0], sum(GROUPS[q]))
        rows = [pl.ds(pl.multiple_of(chip_at(*place) * CHIP_ROWS, CHIP_ROWS), CHIP_ROWS) for place in chips]
        for own in rows:
            wq[own, group] = (wraw[q][own].astype(F32) * scales[0, 0:1, group]).astype(BF16)

        @pl.loop(0, 2)
        def _(m):
            toks = pl.ds(pl.multiple_of(m * TOK, TOK), TOK)
            left = jnp.concatenate([xs[toks, own] for own in rows], axis=1)
            right = jnp.concatenate([wq[own, group] for own in rows], axis=0)
            part = jnp.dot(left, right, preferred_element_type=F32)
            h[toks, group] = part if fresh else h[toks, group] + part

    def chunks_near(q):
        chunks(q, ((0, 0), (1, 0), (3, 0), (0, 1), (0, 3)), fresh=True)

    def chunks_corner(q):
        chunks(q, ((1, 1), (1, 3), (3, 1), (3, 3)))

    def chunks_across(q, a):
        chunks(q, ((2, a), (a, 2)))

    low_tok = lax.broadcasted_iota(jnp.int32, (64, 128), 1) < 64

    def activation_grads(gate, up, cot):
        sig = jax.nn.sigmoid(gate)
        return cot * up * sig * (1.0 + gate * (1.0 - sig)), cot * gate * sig

    def hidden_grads(q):
        @pl.loop(0, 2 * TOK // 64)
        def _(m):
            toks = pl.ds(pl.multiple_of(m * 64, 64), 64)
            start, width = GROUPS[q]
            inv = scales[1, 0:1, start : start + width]
            hidden = h[toks, start : start + width] * inv
            main = 256 if q == 0 else 128
            cot = cots[toks, pl.ds(pl.multiple_of(c * 512 + 256 * q, 128), main)].astype(F32)
            dgate, dup = activation_grads(hidden[:, 0:main], hidden[:, main : 2 * main], cot)
            parts = [(0, main, dgate), (main, 2 * main, dup)]
            if q == 1:
                mixed = hidden[:, 256:384]
                block = cots[toks, MAIN : MAIN + 128].astype(F32)
                block = jnp.where(c == 0, block, pltpu.roll(block, 64, 1))
                mgate, mup = activation_grads(mixed, pltpu.roll(mixed, 64, 1), block)
                parts.append((256, 384, jnp.where(low_tok, mgate, pltpu.roll(mup, 64, 1))))
            for lo, hi, part in parts:
                g[toks, start + lo : start + hi] = part.astype(BF16)
                gs[toks, start + lo : start + hi] = (part * inv[:, lo:hi]).astype(BF16)

    def weight_grad(q, r, a, b):
        group = slice(GROUPS[q][0], sum(GROUPS[q]))
        return jnp.dot(xt[pl.ds(row_of(r, a, b), ROWS)], g[:, group], preferred_element_type=F32)

    def toward(r, axis, sign):
        return at(*place(r, *((sign % SIDE, 0) if axis == 0 else (0, sign % SIDE))))

    def s1_copy(q, r, a, part):
        return remote(
            s1buf[q].at[r, a, pl.ds(part * HALF, HALF)], s1in[q].at[r, a, part],
            s1_send.at[q, r, a, part], s1_recv.at[q, r, a, part], toward(r, 1, 1 - 2 * part),
        )

    def s2_copy(q, r, a, part):
        return remote(
            s2buf[q].at[r, a, part], s2in[q].at[r, a, part],
            s2_send.at[q, r, a, part], s2_recv.at[q, r, a, part], toward(r, 1, 1 - 2 * part),
        )

    def t1_copy(q, r, part):
        return remote(
            rbuf[q].at[r, 2, pl.ds(part * HALF, HALF)], t1in[q].at[r, part],
            t1_send.at[q, r, part], t1_recv.at[q, r, part], toward(r, 0, 1 - 2 * part),
        )

    def t2_copy(q, r, part):
        return remote(
            rbuf[q].at[r, 1 + 2 * part], t2in[q].at[r, part],
            t2_send.at[q, r, part], t2_recv.at[q, r, part], toward(r, 0, 1 - 2 * part),
        )

    def step1(q):
        for a in (2, 1, 3, 0):
            for r in (0, 1):
                s1buf[q][r, a] = weight_grad(q, r, a, 2).astype(BF16)
                s1_copy(q, r, a, 0).start()
                s1_copy(q, r, a, 1).start()

    chunks_near(0)
    first_forward(1)
    chunks_corner(0)
    second_end(0, 0)
    second_forward(0, 2)
    chunks_across(0, 0)
    second_forward(1, 0)
    chunks_near(1)
    for a in (1, 3):
        second_end(0, a)
        chunks_across(0, a)
    first_end(1)
    second_end(0, 2)
    chunks(0, ((2, 2),))
    hidden_grads(0)
    second_forward(1, 1)
    second_forward(1, 3)
    chunks_corner(1)
    second_end(1, 0)
    chunks_across(1, 0)
    second_forward(1, 2)
    step1(0)
    for a in (1, 3):
        second_end(1, a)
        chunks_across(1, a)
    second_end(1, 2)
    chunks(1, ((2, 2),))
    hidden_grads(1)
    step1(1)

    def p_copy(dz):
        return remote(p_send.at[dz], p_in.at[dz], p_ssem.at[dz], p_rsem.at[dz], sibling)

    def input_grads(k):
        odd = lax.rem(k, 2)
        dz = odd * (4 - lax.div(k + 1, 2)) + (1 - odd) * (4 + lax.div(k, 2))
        cols = pl.ds(pl.multiple_of(lax.rem(z + dz, DEPTH) * ZCOL, ZCOL), ZCOL)
        p_send[dz] = lax.dot_general(gs[TOK:, :], wq[cols], NT, preferred_element_type=F32).astype(BF16)
        p_copy(dz).start()
        p_own[dz] = lax.dot_general(gs[:TOK, :], wq[cols], NT, preferred_element_type=F32).astype(BF16)

    def added(out, total, part, extra):
        lo = slice(part * HALF, part * HALF + HALF)
        hi = slice((1 - part) * HALF, (1 - part) * HALF + HALF)
        out[lo] = (total[lo] + extra.astype(F32)).astype(BF16)
        out[hi] = total[hi].astype(BF16)

    def step2(a, halves=(0, 1), groups=(0, 1)):
        for q in groups:
            for r in halves:
                for part in (0, 1):
                    grad = weight_grad(q, r, a, 1 + 2 * part)
                    s1_copy(q, r, a, part).wait_recv()
                    added(s2buf[q].at[r, a, part], grad, part, s1in[q][r, a, part])
                    s2_copy(q, r, a, part).start()

    def reduced(q, r, a):
        grad = weight_grad(q, r, a, 0)
        s2_copy(q, r, a, 0).wait_recv()
        s2_copy(q, r, a, 1).wait_recv()
        return grad + s2in[q][r, a, 0].astype(F32) + s2in[q][r, a, 1].astype(F32)

    def z1_copy(part):
        return remote(
            p_own.at[4, pl.ds(part * (TOK // 2), TOK // 2)], z1in.at[part],
            z1_send.at[part], z1_recv.at[part], at_z(1 if part == 0 else DEPTH - 1),
        )

    def z_copy(step, part):
        dz = (3 - step) if part == 0 else (5 + step)
        return remote(
            p_own.at[dz], zin.at[step, part],
            z_send.at[step, part], z_recv.at[step, part], at_z(1 if part == 0 else DEPTH - 1),
        )

    def pair_sum(dz):
        p_copy(dz).wait_recv()
        return p_own[dz].astype(F32) + p_in[dz].astype(F32)

    def z_first():
        p_own[4] = pair_sum(4).astype(BF16)
        z1_copy(0).start()
        z1_copy(1).start()

    def z_round(step):
        for part in (0, 1):
            dz = (3 - step) if part == 0 else (5 + step)
            total = pair_sum(dz)
            if step == 0:
                z1_copy(part).wait_recv()
                lo = slice(part * (TOK // 2), (part + 1) * (TOK // 2))
                hi = slice((1 - part) * (TOK // 2), (2 - part) * (TOK // 2))
                p_own[dz, lo] = (total[lo] + z1in[part].astype(F32)).astype(BF16)
                p_own[dz, hi] = total[hi].astype(BF16)
            else:
                z_copy(step - 1, part).wait_recv()
                p_own[dz] = (total + zin[step - 1, part].astype(F32)).astype(BF16)
            z_copy(step, part).start()

    def reduced_across(q):
        for r in (0, 1):
            rbuf[q][r, 2] = reduced(q, r, 2).astype(BF16)
            t1_copy(q, r, 0).start()
            t1_copy(q, r, 1).start()

    def later(q, r, part):
        total = reduced(q, r, 1 + 2 * part)
        t1_copy(q, r, part).wait_recv()
        added(rbuf[q].at[r, 1 + 2 * part], total, part, t1in[q][r, part])
        t2_copy(q, r, part).start()

    pl.loop(0, 1)(input_grads)
    step2(2)
    z_first()
    pl.loop(1, 3)(input_grads)
    step2(1)
    z_round(0)
    pl.loop(3, 5)(input_grads)
    reduced_across(0)
    reduced_across(1)
    step2(3)
    z_round(1)
    pl.loop(5, DEPTH)(input_grads)
    for q in (0, 1):
        swap_copy(q, own_rows).wait_send()
    tok_pair.wait_send()
    cot_pair.wait_send()
    for copy in started:
        copy.wait_send()
    for stage in range(len(stages)):
        for copy in am_copies(stage):
            copy.wait_send()
    step2(0, (1,))
    step2(0, (0,), (0,))
    for part in (0, 1):
        for q in (0, 1):
            later(q, 1, part)
    step2(0, (0,), (1,))
    z_round(2)
    for part in (0, 1):
        for q in (0, 1):
            later(q, 0, part)

    def finished(q, r):
        total = reduced(q, r, 0)
        t2_copy(q, r, 0).wait_recv()
        t2_copy(q, r, 1).wait_recv()
        return (total + t2in[q][r, 0].astype(F32) + t2in[q][r, 1].astype(F32)).astype(BF16)

    def last_copy(q):
        return remote(final[q].at[1], final_in[q], pair_send.at[4 + q], pair_recv.at[4 + q], sibling)

    for q in (0, 1):
        for r in (0, 1):
            for part in (0, 1):
                for a in range(SIDE):
                    s1_copy(q, r, a, part).wait_send()
                    if a or r:
                        s2_copy(q, r, a, part).wait_send()
                t1_copy(q, r, part).wait_send()
    for part in (0, 1):
        t2_copy(0, 1, part).wait_send()
        t2_copy(1, 1, part).wait_send()
        z1_copy(part).wait_send()
        z_copy(0, part).wait_send()
        z_copy(1, part).wait_send()
    for dz in range(DEPTH):
        p_copy(dz).wait_send()

    for q in (0, 1):
        final[q][1] = finished(q, 1)
        last_copy(q).start()
    total = pair_sum(0)
    z_copy(2, 0).wait_recv()
    z_copy(2, 1).wait_recv()
    ig_ref[...] = (total + zin[2, 0].astype(F32) + zin[2, 1].astype(F32)).astype(BF16)
    ig_out = pltpu.make_async_copy(ig_ref, ig_hbm, loc_sem.at[4])
    ig_out.start()
    outs = [amax_out, ig_out]
    for q, (own_hbm, other_hbm) in enumerate(((own0_hbm, other0_hbm), (own1_hbm, other1_hbm))):
        last_copy(q).wait_recv()
        outs.append(pltpu.make_async_copy(final_in[q], other_hbm, loc_sem.at[5 + q]))
        outs[-1].start()
        final[q][0] = finished(q, 0)
        outs.append(pltpu.make_async_copy(final[q].at[0], own_hbm, loc_sem.at[8 + q]))
        outs[-1].start()

    for q in (0, 1):
        last_copy(q).wait_send()
        for part in (0, 1):
            t2_copy(q, 0, part).wait_send()
            s2_copy(q, 0, 0, part).wait_send()
    for part in (0, 1):
        z_copy(2, part).wait_send()
    for copy in outs:
        copy.wait()


def hand_over(ig_in, own0, own1, other0, other1, amax_in, ig_out, gg_out, ug_out, amax_out):
    c = lax.rem(lax.axis_index("fsdp"), 2)
    low = lax.broadcasted_iota(jnp.int32, (ROWS, 128), 1) < 64
    ig_out[...] = ig_in[...]

    def placed(group0, group1, first):
        cols = pl.ds(first, 256)
        gg_out[:, cols] = group0[:, 0:256]
        ug_out[:, cols] = group0[:, 256:512]
        cols = pl.ds(pl.multiple_of(first + 256, 128), 128)
        gg_out[:, cols] = group1[:, 0:128]
        ug_out[:, cols] = group1[:, 128:256]
        return group1[:, 256:384].astype(F32)

    mine = placed(own0, own1, pl.multiple_of(c * 512, 128))
    theirs = placed(other0, other1, pl.multiple_of((1 - c) * 512, 128))
    first = jnp.where(c == 0, mine, theirs)
    second = jnp.where(c == 0, theirs, mine)
    gg_out[:, MAIN : MAIN + 128] = jnp.where(low, first, pltpu.roll(second, 64, 1)).astype(BF16)
    ug_out[:, MAIN : MAIN + 128] = jnp.where(low, pltpu.roll(first, 64, 1), second).astype(BF16)
    amax_out[0] = jnp.max(amax_in[0:4, :])
    amax_out[1] = jnp.max(amax_in[4:8, :])


def on_device(tokens, cotangent, gate_weight, up_weight):
    vmem = pltpu.VMEM
    dma = pltpu.SemaphoreType.DMA

    def both(*shape):
        return tuple(vmem(shape + (width,), BF16) for _, width in GROUPS)

    scratch = [
        vmem((ROWS, WIDTH), BF16),
        vmem((ROWS, WIDTH), BF16),
        vmem((TOK, ZCOL), BF16),
        vmem((2 * TOK, D), BF16),
        vmem((D, 2 * TOK), BF16),
        vmem((2 * TOK, WIDTH), BF16),
        both(D),
        vmem((D, WIDTH), BF16),
        vmem((2 * TOK, WIDTH), F32),
        vmem((2 * TOK, WIDTH), BF16),
        vmem((2 * TOK, WIDTH), BF16),
        both(ROWS),
        vmem((2, 8, WIDTH), F32),
        vmem((5, 8, 128), F32),
        vmem((14, 8, 128), F32),
        both(2, SIDE, ROWS),
        both(2, SIDE, 2, HALF),
        both(2, SIDE, 2, ROWS),
        both(2, SIDE, 2, ROWS),
        both(2, SIDE, ROWS),
        both(2, 2, HALF),
        both(2, 2, ROWS),
        both(2, ROWS),
        both(ROWS),
        vmem((DEPTH, TOK, ZCOL), BF16),
        vmem((DEPTH, TOK, ZCOL), BF16),
        vmem((DEPTH, TOK, ZCOL), BF16),
        vmem((2, TOK // 2, ZCOL), BF16),
        vmem((3, 2, TOK, ZCOL), BF16),
        dma((10,)), dma((6,)), dma((6,)), dma((2, 2, 20)), dma((2, 2, 20)), dma((14,)), dma((14,)),
        dma((2, 2, SIDE, 2)), dma((2, 2, SIDE, 2)), dma((2, 2, SIDE, 2)), dma((2, 2, SIDE, 2)),
        dma((2, 2, 2)), dma((2, 2, 2)), dma((2, 2, 2)), dma((2, 2, 2)),
        dma((DEPTH,)), dma((DEPTH,)), dma((2,)), dma((2,)), dma((3, 2)), dma((3, 2)),
    ]
    anywhere = pl.BlockSpec(memory_space=pl.ANY)
    scalars = pl.BlockSpec(memory_space=pltpu.SMEM)
    whole = pl.BlockSpec(memory_space=pltpu.VMEM)
    outs = pl.pallas_call(
        kernel,
        out_shape=(
            jax.ShapeDtypeStruct((TOK, ZCOL), BF16),
            jax.ShapeDtypeStruct((ROWS, GROUPS[0][1]), BF16),
            jax.ShapeDtypeStruct((ROWS, GROUPS[1][1]), BF16),
            jax.ShapeDtypeStruct((ROWS, GROUPS[0][1]), BF16),
            jax.ShapeDtypeStruct((ROWS, GROUPS[1][1]), BF16),
            jax.ShapeDtypeStruct((8, 128), F32),
        ),
        in_specs=[anywhere] * 4,
        out_specs=(anywhere,) * 6,
        scratch_shapes=scratch,
        compiler_params=pltpu.CompilerParams(
            collective_id=0, has_side_effects=True, vmem_limit_bytes=62 * 1024 * 1024
        ),
        cost_estimate=pl.CostEstimate(flops=3 * 2 * 512 * 4096 * 896, bytes_accessed=4 << 20, transcendentals=512 * 448),
        name="swiglu_backward",
    )(tokens, cotangent, gate_weight, up_weight)
    return pl.pallas_call(
        hand_over,
        out_shape=(
            jax.ShapeDtypeStruct((TOK, ZCOL), BF16),
            jax.ShapeDtypeStruct((ROWS, WIDTH), BF16),
            jax.ShapeDtypeStruct((ROWS, WIDTH), BF16),
            jax.ShapeDtypeStruct((2,), F32),
        ),
        in_specs=[whole] * 6,
        out_specs=(whole,) * 3 + (scalars,),
        compiler_params=pltpu.CompilerParams(vmem_limit_bytes=62 * 1024 * 1024),
        name="hand_over",
    )(*outs)


def solution(mesh):
    in_specs = (P("fsdp", None), P("fsdp", "tp"), P("fsdp", "tp"), P("fsdp", "tp"))
    out_specs = (P("fsdp", "tp"), P("fsdp", "tp"), P("fsdp", "tp"), P())
    return jax.shard_map(
        on_device, mesh=mesh, in_specs=in_specs, out_specs=out_specs, check_vma=False
    )
```
